128 devices in a mesh: seq: 4 (over x), head: 32 (over z, y, core).
Axes of the slice: x: 4, y: 4, z: 4, core: 2. Of those that a mesh axis runs over, the one named last changes fastest.
Arguments:
- tokens: bfloat16 [2048, 2048], P('seq'), may hold values from -40 to 40
- attention_gain: float32 [2048], replicated, may hold values from 0.1 to 1.9
- head_weights: bfloat16 [3, 2048, 2048], P(None, None, 'head'), may hold values from -1 to 1
- carried_state: float32 [8256, 2048], P(None, 'head'), may hold values from -384 to 384
- output_weight: bfloat16 [2048, 2048], P('head'), may hold values from -0.125 to 0.125
- expert_gain: float32 [2048], replicated, may hold values from 0.1 to 1.9
- router_weight: bfloat16 [2048, 64], replicated, may hold values from -0.125 to 0.125
- expert_index: int32 [2048, 8], P(('seq', 'head')), may hold values from 0 to 63, all different within a row; in each aligned block of 16 rows (0 to 15, 16 to 31, ...) at most 3 rows name the same one
- expert_first: bfloat16 [2, 2048, 65536], P(None, None, ('seq', 'head')), may hold values from -0.125 to 0.125
- expert_second: bfloat16 [65536, 2048], P(('seq', 'head')), may hold values from -0.1875 to 0.1875
Outputs:
- layer_out: bfloat16 [2048, 2048], P(('seq', 'head'))
The draws below stay inside these ranges and needn't reach their ends.
Inputs may be any that keep to these rules, and one draw needn't show every extreme that they name: `expert_index`: each row names 8 different experts; within each aligned block of 16 rows (the rows of one device) no expert is named by more than 3 rows.
All inputs are finite; a program needn't handle non-finite values.
Results may differ from the reference program's by a relative error of at most 0.019.
Values may be sent and summed in bfloat16 or wider, within the bound.
No kernel may reach another device: no remote copies, remote signals or barrier semaphores. Data moves between devices by JAX's collectives and lax.ppermute only.
A program may use at most 128 MiB of HBM per device.

```python
import math
import jax
import jax.numpy as jnp
import numpy as np
from jax import lax

HD = 128
HEADS = 16
D = 2048
STATE = 8256
EXPERTS = 64
TOP = 8
FF = 1024
TOK_SEQ = 512
TOKENS = 2048
SLAB = 16
CAP = 3
SPLIT = 2
N_SEQ = 4


def draw_tokens(key, part):
    key = jax.random.fold_in(key, 11)
    jitter_key, row_key, column_key = jax.random.split(key, 3)
    jitter = jax.random.truncated_normal(jitter_key, -4.0, 4.0, (TOKENS, D), jnp.float32)
    row_scale = jnp.exp(jax.random.uniform(row_key, (TOKENS, 1), jnp.float32, math.log(0.3), math.log(3.0)))
    column_scale = jnp.exp(jax.random.uniform(column_key, (1, D), jnp.float32, -0.5 * math.log(10.0), 0.5 * math.log(10.0)))
    return (row_scale * (jitter * column_scale)).astype(jnp.bfloat16)


def draw_head_weights(key, part):
    key = jax.random.fold_in(key, 23)
    entry_key, column_key = jax.random.split(key)
    entries = jax.random.truncated_normal(entry_key, -4.0, 4.0, (3, D, D), jnp.float32)
    column_scale = jnp.exp(jax.random.uniform(column_key, (3, 1, D), jnp.float32, -0.5 * math.log(10.0), 0.5 * math.log(10.0)))
    return (entries * column_scale / math.sqrt(D)).astype(jnp.bfloat16)


def level_of(key, extent, cuts, least, high):
    level = 1.0
    for position, blocks in cuts:
        draws = jax.random.uniform(jax.random.fold_in(jax.random.fold_in(key, 6), position), (blocks,), jnp.float32, least / len(cuts), high / len(cuts))
        level = level * jnp.repeat(jnp.exp(draws), extent[position] // blocks).reshape((-1,) + (1,) * (len(extent) - 1 - position))
    return level


def shared_out(own_key, own, number, rows, number_of, top, most, lean):
    order = jax.random.permutation(own_key, number_of)
    crowded, usual = load_shares(number_of, rows * top, most, lean, True), load_shares(number_of, rows * top, most, lean, False)
    places = jnp.arange(number_of)

    def named(sizes, rotation):
        used = int((sizes > 0).sum())
        fixed = max(1, used // 4)
        passed = fixed + (places - fixed + rotation * (used - fixed)) % max(1, number_of - fixed)
        return jnp.zeros((number_of,), jnp.int32).at[order[jnp.where(places < fixed, places, passed)]].set(jnp.asarray(sizes, jnp.int32))

    sizes = jnp.where(number % 4 == 0, named(crowded, number // 4), named(usual, number - number // 4 - 1))
    mixed = jax.random.permutation(jax.random.fold_in(own, 3), number_of)
    source_of, receiver = mixed[0:number_of // 2 * 2:2], mixed[1:number_of // 2 * 2:2]
    margin = jnp.minimum(sizes[source_of] - 1, most - sizes[receiver]) // 2
    margin = jnp.where((source_of == order[0]) | (receiver == order[0]) | (sizes[receiver] == 0), 0, jnp.maximum(margin, 0))
    passed = jax.random.randint(jax.random.fold_in(own, 4), (number_of // 2,), 0, 1 << 20) % (margin + 1)
    sizes = sizes.at[source_of].add(-passed).at[receiver].add(passed)
    members = jnp.searchsorted(jnp.cumsum(sizes), jnp.arange(rows * top), side="right").astype(jnp.int32)
    grid = members.reshape(top, rows).T
    grid = grid[jax.random.permutation(jax.random.fold_in(own, 1), rows)]
    rotation = jax.random.randint(jax.random.fold_in(own, 2), (rows, 1), 0, top)
    return jnp.take_along_axis(grid, (jnp.arange(top)[None, :] + rotation) % top, axis=1)


def load_shares(count, total, most, skew, full):
    loads = [(1 << 20) // math.isqrt(grade ** skew) + 1 for grade in range(1, count + 1)]
    largest = most if full else min(most, max(-(-total // count), total * loads[0] // sum(loads)))
    least = 1 if total - largest >= count - 1 else 0
    counts, spare = [largest] + [least] * (count - 1), total - largest - least * (count - 1)
    while spare > 0:
        movable = [i for i in range(1, count) if counts[i] < largest] or [i for i in range(1, count) if counts[i] < most]
        pool, left = sum([loads[i] for i in movable]), spare
        for i in movable:
            extra = min(most - counts[i], max(1, left * loads[i] // pool), spare)
            counts[i] = counts[i] + extra
            spare = spare - extra
    return np.array(counts)


def normal_values(key, dims, scale, bound, cuts=(), kind=jnp.bfloat16):
    drawn = jax.random.normal(key, dims, jnp.float32) * scale
    if len(cuts) > 0:
        drawn = level_of(key, dims, cuts, -0.22, 0.18) * drawn
    return jnp.clip(drawn, min=-bound, max=bound).astype(kind)


def setup_inputs(seed: int = 0) -> dict:
    key_list = jax.random.split(jax.random.key(seed), 11)
    tokens = draw_tokens(jax.random.fold_in(key_list[10], 71), 0)
    attention_gain = jnp.clip(1.0 + 0.18 * jax.random.normal(key_list[1], (D,), jnp.float32), 0.1, 1.9)
    head_weights = draw_head_weights(jax.random.fold_in(key_list[10], 71), 0)
    carried_state = normal_values(key_list[3], (STATE, D), 64.0, 384.0, ((1, 32),), jnp.float32)
    output_weight = normal_values(key_list[4], (D, D), D ** -0.5, 0.125, ((0, 32),))
    expert_gain = jnp.clip(1.0 + 0.18 * jax.random.normal(key_list[5], (D,), jnp.float32), 0.1, 1.9)
    router_weight = normal_values(key_list[6], (D, EXPERTS), D ** -0.5, 0.125)
    expert_index_keys = jax.random.split(jax.random.fold_in(key_list[7], 1), TOKENS // SLAB)
    expert_index_turns = jax.random.permutation(jax.random.fold_in(key_list[7], 3), TOKENS // SLAB)
    expert_index = jax.vmap(lambda own, number: shared_out(jax.random.fold_in(key_list[7], 2), own, number, SLAB, EXPERTS, TOP, CAP, 2))(expert_index_keys, expert_index_turns).reshape((TOKENS, TOP))
    expert_first = normal_values(key_list[8], (2, D, EXPERTS * FF), D ** -0.5, 0.125, ((2, 128),))
    expert_second = normal_values(key_list[9], (EXPERTS * FF, D), FF ** -0.5, 0.1875, ((0, 128),))
    return dict(tokens=tokens, attention_gain=attention_gain, head_weights=head_weights, carried_state=carried_state, output_weight=output_weight, expert_gain=expert_gain, router_weight=router_weight, expert_index=expert_index, expert_first=expert_first, expert_second=expert_second)


def features(vectors):
    breadth = vectors.shape[1]
    pieces = []
    for column in range(breadth):
        factors = np.concatenate([np.ones((1,), np.float32), np.full((breadth - column - 1,), math.sqrt(2.0), np.float32)])
        pieces.append(vectors[:, column:column + 1] * (vectors[:, column:] * factors))
    return jnp.concatenate(pieces, axis=1)

def norm_scaled(values, gain):
    return values * lax.rsqrt(lax.optimization_barrier(jnp.mean(values * values, axis=-1, keepdims=True)) + 1e-06) * gain

def head_output(operands):
    query_rows, key_rows, value_rows, memory = operands
    value_float = value_rows.astype(jnp.float32)
    key_place = jnp.arange(TOKENS, dtype=jnp.int32)

    def block_output(block_num):
        offset = (block_num * TOK_SEQ).astype(jnp.int32)
        query_block = lax.dynamic_slice_in_dim(query_rows, offset, TOK_SEQ, 0)
        scores = lax.dot_general(query_block, key_rows, (((1,), (1,)), ((), ())), preferred_element_type=jnp.float32)
        query_place = offset + jnp.arange(TOK_SEQ, dtype=jnp.int32)
        weights = jnp.where(key_place[None, :] <= query_place[:, None], scores * scores, 0.0)
        nearby = jnp.dot(weights, value_float, precision=lax.Precision.HIGHEST)
        lifted = features(query_block.astype(jnp.float32))
        carried = jnp.dot(lifted, memory, precision=lax.Precision.HIGHEST)
        return (nearby + carried) / HD
    outputs = lax.map(block_output, jnp.arange(N_SEQ, dtype=jnp.int32))
    return outputs.reshape(TOKENS, HD)

def reference(tokens, attention_gain, head_weights, carried_state, output_weight, expert_gain, router_weight, expert_index, expert_first, expert_second):
    floats = tokens.astype(jnp.float32)
    normed = norm_scaled(floats, attention_gain).astype(jnp.bfloat16)
    query_rows = jnp.dot(normed, head_weights[0], preferred_element_type=jnp.float32).astype(jnp.bfloat16)
    key_rows = jnp.dot(normed, head_weights[1], preferred_element_type=jnp.float32).astype(jnp.bfloat16)
    value_rows = jnp.dot(normed, head_weights[2], preferred_element_type=jnp.float32).astype(jnp.bfloat16)

    def by_head(matrix):
        return matrix.reshape(TOKENS, HEADS, HD).transpose(1, 0, 2)
    memories = carried_state.reshape(STATE, HEADS, HD).transpose(1, 0, 2)
    raw_heads = lax.map(head_output, (by_head(query_rows), by_head(key_rows), by_head(value_rows), memories))
    attended = norm_scaled(raw_heads, 1.0).astype(jnp.bfloat16).transpose(1, 0, 2).reshape(TOKENS, D)
    residual = floats + jnp.dot(attended, output_weight, preferred_element_type=jnp.float32)
    expert_input = norm_scaled(residual, expert_gain).astype(jnp.bfloat16)
    logits = jnp.dot(expert_input, router_weight, preferred_element_type=jnp.float32)
    gate_values = jax.nn.sigmoid(jnp.take_along_axis(logits, expert_index, axis=1))
    flat_index = expert_index.reshape(TOKENS * TOP)
    flat_gates = gate_values.reshape(TOKENS * TOP)
    owners = (jnp.arange(TOKENS * TOP, dtype=jnp.int32) // TOP).astype(jnp.int32)
    capacity_rows = TOKENS // SLAB * CAP
    piece_width = FF // SPLIT

    def expert_step(running, expert):
        chosen = flat_index == expert
        places = (jnp.cumsum(chosen.astype(jnp.int32)) - 1).astype(jnp.int32)
        targets = jnp.where(chosen, places, capacity_rows).astype(jnp.int32)
        row_ids = jnp.zeros((capacity_rows,), jnp.int32).at[targets].set(owners, mode='drop')
        weights = jnp.zeros((capacity_rows,), jnp.float32).at[targets].set(flat_gates, mode='drop')
        inputs = jnp.take(expert_input, row_ids, axis=0)
        first_cols = lax.dynamic_slice_in_dim(expert_first, (expert * FF).astype(jnp.int32), FF, 2)
        gate_part = jnp.dot(inputs, first_cols[0], preferred_element_type=jnp.float32)
        up_part = jnp.dot(inputs, first_cols[1], preferred_element_type=jnp.float32)
        hidden = (jax.nn.silu(gate_part) * up_part).astype(jnp.bfloat16)
        outputs = jnp.zeros((capacity_rows, D), jnp.float32)
        for portion in range(SPLIT):
            down_rows = lax.dynamic_slice_in_dim(expert_second, (expert * FF + portion * piece_width).astype(jnp.int32), piece_width, 0)
            product = jnp.dot(hidden[:, portion * piece_width:(portion + 1) * piece_width], down_rows, preferred_element_type=jnp.float32)
            rounded = lax.optimization_barrier(product.astype(jnp.bfloat16))
            outputs = outputs + rounded.astype(jnp.float32)
        return (running.at[row_ids].add(weights[:, None] * outputs), None)
    expert_sum, unused = lax.scan(expert_step, jnp.zeros((TOKENS, D), jnp.float32), jnp.arange(EXPERTS, dtype=jnp.int32))
    return (residual + expert_sum).astype(jnp.bfloat16)
```

```python
import functools
import math

import jax
import jax.numpy as jnp
from jax import lax
from jax.experimental import pallas as pl
from jax.experimental.pallas import tpu as pltpu
from jax.sharding import Mesh
from jax.sharding import PartitionSpec as P

HD = 128
D = 2048
STATE = 8256
EXPERTS = 64
TOP = 8
CAP = 3
SLAB = 16
HALF = 256
SHARD = 512
CHIP_AXES = ("x", "z", "y")


def swap_core(array):
    return lax.ppermute(array, "c", [(0, 1), (1, 0)])


def shift(array, axis, step):
    return lax.ppermute(array, axis, [(i, (i + step) % 4) for i in range(4)])


def norm_scaled(values, gain):
    return values * lax.rsqrt(jnp.mean(values * values, axis=-1, keepdims=True) + 1e-06) * gain


GROUP = 8
LOOPED = 112
TAIL_AT = 8064


def carried_kernel(m_ref, q_own_ref, q_other_ref, out_ref, q_ref, w_ref, tail_ref):
    q_ref[:, :HALF] = q_own_ref[...].astype(jnp.float32)
    q_ref[:, HALF:] = q_other_ref[...].astype(jnp.float32)
    tail_ref[:, : STATE - TAIL_AT] = m_ref[:, TAIL_AT:]
    q_cols = jnp.concatenate([q_own_ref[...], q_other_ref[...]], axis=1)
    lane = lax.broadcasted_iota(jnp.int32, (64, 128), 1)
    root = math.sqrt(2.0)

    def piece(first, second, turn, i):
        joined = jnp.where(
            lane < 128 - turn,
            pltpu.roll(first, (128 - turn) % 128, 1),
            pltpu.roll(second, (128 - turn) % 128, 1),
        )
        return jnp.where(lane > i, joined * root, jnp.where(lane == i, joined, 0.0)).astype(
            jnp.bfloat16
        )

    def finish(rows):
        spread = jnp.dot(w_ref[...], q_cols, preferred_element_type=jnp.float32)
        total = spread[0:64] * rows[0]
        for k in range(1, GROUP):
            total = total + spread[64 * k : 64 * k + 64] * rows[k]
        return total

    out_ref[...] = jnp.zeros_like(out_ref)

    def group(g, carry):
        base = g * GROUP
        for k in range(GROUP):
            i = base + k
            offset = 127 * i - (i * (i - 1)) // 2
            tile = pl.multiple_of((offset // 128) * 128, 128)
            w_ref[64 * k : 64 * k + 64, :] = piece(
                m_ref[:, pl.ds(tile, 128)],
                m_ref[:, pl.ds(pl.multiple_of(tile + 128, 128), 128)],
                offset - tile,
                i,
            )
        out_ref[...] += finish([q_ref[pl.ds(base + k, 1), :] for k in range(GROUP)])
        return carry

    lax.fori_loop(0, LOOPED // GROUP, group, 0)
    for base in range(LOOPED, HD, GROUP):
        for k in range(GROUP):
            i = base + k
            offset = 127 * i - (i * (i - 1)) // 2
            tile = (offset // 128) * 128
            if tile < TAIL_AT:
                first, second = m_ref[:, tile : tile + 128], m_ref[:, tile + 128 : tile + 256]
            else:
                first, second = tail_ref[:, :128], tail_ref[:, 128:]
            w_ref[64 * k : 64 * k + 64, :] = piece(first, second, offset - tile, i)
        out_ref[...] += finish([q_ref[base + k : base + k + 1, :] for k in range(GROUP)])


def carried_part(state_cols, q_own, q_other):
    return pl.pallas_call(
        carried_kernel,
        out_shape=jax.ShapeDtypeStruct((64, SHARD), jnp.float32),
        in_specs=[pl.BlockSpec(memory_space=pltpu.VMEM)] * 3,
        out_specs=pl.BlockSpec(memory_space=pltpu.VMEM),
        scratch_shapes=[
            pltpu.VMEM((HD, SHARD), jnp.float32),
            pltpu.VMEM((64 * GROUP, HD), jnp.bfloat16),
            pltpu.VMEM((64, 256), jnp.float32),
        ],
        compiler_params=pltpu.CompilerParams(vmem_limit_bytes=32 * 1024 * 1024),
        cost_estimate=pl.CostEstimate(
            flops=8192 * 512 * 128 * 4, bytes_accessed=64 * STATE * 4, transcendentals=0
        ),
        name="carried",
    )(state_cols, q_own, q_other)


def window_kernel(core_ref, q_own_ref, q_other_ref, kv0, kv1, kv2, kv3, carried_ref, mine_ref, send_ref):
    core = core_ref[0]
    q_cols = jnp.concatenate([q_own_ref[...], q_other_ref[...]], axis=1)
    key = lax.broadcasted_iota(jnp.int32, (HALF, SHARD), 0)
    query = lax.broadcasted_iota(jnp.int32, (HALF, SHARD), 1)
    key_place = (key // 16) * 32 + key % 16 + core * 16
    inside = query % HALF
    query_place = (inside // 16) * 32 + inside % 16 + jnp.where(query < HALF, core, 1 - core) * 16
    allowed = key_place <= query_place
    total = jnp.zeros((HD, SHARD), jnp.float32)
    for number, kv in enumerate((kv0, kv1, kv2, kv3)):
        scores = lax.dot_general(
            kv[:HD, :], q_cols, (((0,), (0,)), ((), ())), preferred_element_type=jnp.float32
        )
        weights = scores * scores
        if number == 0:
            weights = jnp.where(allowed, weights, 0.0)
        total = total + jnp.dot(
            kv[HD:, :], weights.astype(jnp.bfloat16), preferred_element_type=jnp.float32
        )
    upper = total[:64] + carried_ref[...]
    lower = total[64:]
    mine_ref[...] = jnp.concatenate([upper[:, :HALF], lower[:, :HALF]], axis=0).T
    send_ref[...] = jnp.concatenate([lower[:, HALF:], upper[:, HALF:]], axis=0).T.astype(jnp.bfloat16)


def window_part(core, q_own, q_other, kvs, carried):
    return pl.pallas_call(
        window_kernel,
        out_shape=(
            jax.ShapeDtypeStruct((HALF, HD), jnp.float32),
            jax.ShapeDtypeStruct((HALF, HD), jnp.bfloat16),
        ),
        in_specs=[pl.BlockSpec(memory_space=pltpu.SMEM)]
        + [pl.BlockSpec(memory_space=pltpu.VMEM)] * 7,
        out_specs=(pl.BlockSpec(memory_space=pltpu.VMEM),) * 2,
        compiler_params=pltpu.CompilerParams(vmem_limit_bytes=32 * 1024 * 1024),
        name="window",
    )(core, q_own, q_other, *kvs, carried)


def body(
    tokens,
    attention_gain,
    head_weights,
    carried_state,
    output_weight,
    expert_gain,
    router_weight,
    expert_index,
    expert_first,
    expert_second,
):
    z, y, c = (lax.axis_index(name) for name in ("z", "y", "c"))
    own_weights = head_weights.transpose(0, 2, 1)
    other_weights = swap_core(own_weights)
    output_own = lax.all_gather(output_weight, "y")
    output_other = swap_core(output_own)

    half_tokens = lax.dynamic_index_in_dim(
        tokens.reshape(16, 2, 16, D), c, axis=1, keepdims=False
    ).reshape(HALF, D)
    normed = norm_scaled(half_tokens.astype(jnp.float32), attention_gain).astype(jnp.bfloat16)

    def project(weights):
        return jnp.einsum("afd,td->aft", weights, normed, preferred_element_type=jnp.float32).astype(
            jnp.bfloat16
        )

    own, other = project(own_weights), project(other_weights)
    lower = jnp.where(c == 0, own[:2], other[:2])
    upper = jnp.where(c == 0, other[:2], own[:2])
    q_own = jnp.concatenate([lower[0], upper[0]])
    kv = jnp.concatenate([lower[1], upper[1], own[2], other[2]])
    q_other = swap_core(q_own)
    kvs = [kv] + [
        lax.ppermute(kv, "x", [(i, i + step) for i in range(4 - step)]) for step in (1, 2, 3)
    ]
    carried = carried_part(carried_state.T, q_own, q_other)
    mine, send = window_part(c.reshape(1), q_own, q_other, kvs, carried)
    raw = (mine + swap_core(send).astype(jnp.float32)) / HD
    attended = norm_scaled(raw, 1.0).astype(jnp.bfloat16)

    by_y = attended.reshape(4, 4, SLAB, HD).transpose(1, 0, 2, 3).reshape(4, 64, HD)

    def block(array, at):
        return lax.dynamic_index_in_dim(array, at % 4, axis=0, keepdims=False)

    pieces = [block(by_y, y)] + [shift(block(by_y, y + step), "y", step) for step in (1, 2, 3)]
    partial = jnp.zeros((64, D), jnp.float32)
    for step in range(4):
        for columns, weights in ((slice(0, 64), output_own), (slice(64, 128), output_other)):
            partial = partial + jnp.dot(
                pieces[step][:, columns],
                block(weights, y - step + 4),
                preferred_element_type=jnp.float32,
            )
    by_z = partial.reshape(4, SLAB, D)
    attention_sum = block(by_z, z)
    by_z = by_z.astype(jnp.bfloat16)
    for step in (1, 2, 3):
        attention_sum = attention_sum + shift(block(by_z, z + step), "z", step).astype(jnp.float32)
    slab = lax.dynamic_slice_in_dim(tokens, ((z * 4 + y) * 2 + c) * SLAB, SLAB, 0)
    residual = slab.astype(jnp.float32) + attention_sum
    expert_input = norm_scaled(residual, expert_gain).astype(jnp.bfloat16)
    logits = jnp.dot(expert_input, router_weight, preferred_element_type=jnp.float32)
    matches = expert_index[:, :, None] == jnp.arange(EXPERTS, dtype=jnp.int32)
    gate_values = jax.nn.sigmoid(jnp.sum(jnp.where(matches, logits[:, None, :], 0.0), axis=2))
    flat_matches = matches.reshape(SLAB * TOP, EXPERTS).astype(jnp.int32)
    earlier = jnp.cumsum(flat_matches, axis=0) - flat_matches
    slots = jnp.sum(earlier * flat_matches, axis=1).reshape(SLAB, TOP)
    cells = EXPERTS * CAP
    hits = (expert_index * CAP + slots)[:, :, None] == jnp.arange(cells, dtype=jnp.int32)
    send_map = jnp.sum(hits.astype(jnp.bfloat16), axis=1)
    combine_map = jnp.sum(jnp.where(hits, gate_values[:, :, None], 0.0), axis=1)
    outgoing = (
        lax.dot_general(
            send_map, expert_input, (((0,), (0,)), ((), ())), preferred_element_type=jnp.float32
        )
        .astype(jnp.bfloat16)
        .reshape(EXPERTS, CAP, D)
    )
    arrived = lax.all_to_all(outgoing, CHIP_AXES, split_axis=0, concat_axis=0, tiled=True).reshape(cells, D)
    arrived_other = swap_core(arrived)

    def expert(rows):
        gate = jnp.dot(rows, expert_first[0], preferred_element_type=jnp.float32)
        up = jnp.dot(rows, expert_first[1], preferred_element_type=jnp.float32)
        hidden = (jax.nn.silu(gate) * up).astype(jnp.bfloat16)
        return jnp.dot(hidden, expert_second, preferred_element_type=jnp.float32)

    back = swap_core(expert(arrived_other).astype(jnp.bfloat16))
    produced = (expert(arrived) + back.astype(jnp.float32)).astype(jnp.bfloat16)
    returned = lax.all_to_all(
        produced.reshape(EXPERTS, CAP, D), CHIP_AXES, split_axis=0, concat_axis=0, tiled=True
    ).reshape(cells, D)
    expert_sum = jnp.dot(
        combine_map.astype(jnp.bfloat16), returned, preferred_element_type=jnp.float32
    )
    return (residual + expert_sum).astype(jnp.bfloat16)


def solution(mesh):
    fine = Mesh(mesh.devices.reshape(4, 4, 4, 2), ("x", "z", "y", "c"))
    head = ("z", "y", "c")
    every = ("x", "z", "y", "c")
    in_specs = (
        P("x", None),
        P(),
        P(None, None, head),
        P(None, head),
        P(head, None),
        P(),
        P(),
        P(every, None),
        P(None, None, every),
        P(every, None),
    )
    return jax.shard_map(body, mesh=fine, in_specs=in_specs, out_specs=P(every, None), check_vma=False)
```

```python
import functools
import math

import jax
import jax.numpy as jnp
from jax import lax
from jax.experimental import pallas as pl
from jax.experimental.pallas import tpu as pltpu
from jax.sharding import Mesh
from jax.sharding import PartitionSpec as P

HD = 128
D = 2048
STATE = 8256
EXPERTS = 64
TOP = 8
CAP = 3
SLAB = 16
HALF = 256
SHARD = 512
CHIP_AXES = ("x", "z", "y")


def swap_core(array):
    return lax.ppermute(array, "c", [(0, 1), (1, 0)])


def shift(array, axis, step):
    return lax.ppermute(array, axis, [(i, (i + step) % 4) for i in range(4)])


def scalars(*values):
    return jnp.stack([jnp.asarray(value, jnp.int32) for value in values])


VMEM = pl.BlockSpec(memory_space=pltpu.VMEM)
SMEM = pl.BlockSpec(memory_space=pltpu.SMEM)
LIMIT = pltpu.CompilerParams(vmem_limit_bytes=32 * 1024 * 1024)
ROWS = EXPERTS * CAP
PIECES = D // 128
TILE_ROWS = ROWS * PIECES


def norm_scaled(values, gain):
    return values * lax.rsqrt(jnp.mean(values * values, axis=-1, keepdims=True) + 1e-06) * gain


GROUP = 8
LOOPED = 112
TAIL_AT = 8064


def carried_kernel(m_ref, q_own_ref, q_other_ref, out_ref, q_ref, w_ref, tail_ref):
    q_ref[:, :HALF] = q_own_ref[...].astype(jnp.float32)
    q_ref[:, HALF:] = q_other_ref[...].astype(jnp.float32)
    tail_ref[:, : STATE - TAIL_AT] = m_ref[:, TAIL_AT:]
    q_cols = jnp.concatenate([q_own_ref[...], q_other_ref[...]], axis=1)
    lane = lax.broadcasted_iota(jnp.int32, (64, 128), 1)
    root = math.sqrt(2.0)

    def piece(first, second, turn, i):
        joined = jnp.where(
            lane < 128 - turn,
            pltpu.roll(first, (128 - turn) % 128, 1),
            pltpu.roll(second, (128 - turn) % 128, 1),
        )
        return jnp.where(lane > i, joined * root, jnp.where(lane == i, joined, 0.0)).astype(
            jnp.bfloat16
        )

    def finish(rows):
        spread = jnp.dot(w_ref[...], q_cols, preferred_element_type=jnp.float32)
        total = spread[0:64] * rows[0]
        for k in range(1, GROUP):
            total = total + spread[64 * k : 64 * k + 64] * rows[k]
        return total

    out_ref[...] = jnp.zeros_like(out_ref)

    def group(g, carry):
        base = g * GROUP
        for k in range(GROUP):
            i = base + k
            offset = 127 * i - (i * (i - 1)) // 2
            tile = pl.multiple_of((offset // 128) * 128, 128)
            w_ref[64 * k : 64 * k + 64, :] = piece(
                m_ref[:, pl.ds(tile, 128)],
                m_ref[:, pl.ds(pl.multiple_of(tile + 128, 128), 128)],
                offset - tile,
                i,
            )
        out_ref[...] += finish([q_ref[pl.ds(base + k, 1), :] for k in range(GROUP)])
        return carry

    lax.fori_loop(0, LOOPED // GROUP, group, 0)
    for base in range(LOOPED, HD, GROUP):
        for k in range(GROUP):
            i = base + k
            offset = 127 * i - (i * (i - 1)) // 2
            tile = (offset // 128) * 128
            if tile < TAIL_AT:
                first, second = m_ref[:, tile : tile + 128], m_ref[:, tile + 128 : tile + 256]
            else:
                first, second = tail_ref[:, :128], tail_ref[:, 128:]
            w_ref[64 * k : 64 * k + 64, :] = piece(first, second, offset - tile, i)
        out_ref[...] += finish([q_ref[base + k : base + k + 1, :] for k in range(GROUP)])


def carried_part(state_cols, q_own, q_other):
    return pl.pallas_call(
        carried_kernel,
        out_shape=jax.ShapeDtypeStruct((64, SHARD), jnp.float32),
        in_specs=[pl.BlockSpec(memory_space=pltpu.VMEM)] * 3,
        out_specs=pl.BlockSpec(memory_space=pltpu.VMEM),
        scratch_shapes=[
            pltpu.VMEM((HD, SHARD), jnp.float32),
            pltpu.VMEM((64 * GROUP, HD), jnp.bfloat16),
            pltpu.VMEM((64, 256), jnp.float32),
        ],
        compiler_params=pltpu.CompilerParams(vmem_limit_bytes=32 * 1024 * 1024),
        cost_estimate=pl.CostEstimate(
            flops=8192 * 512 * 128 * 4, bytes_accessed=64 * STATE * 4, transcendentals=0
        ),
        name="carried",
    )(state_cols, q_own, q_other)


def window_kernel(core_ref, q_own_ref, q_other_ref, kv0, kv1, kv2, kv3, carried_ref, mine_ref, send_ref):
    core = core_ref[0]
    q_cols = jnp.concatenate([q_own_ref[...], q_other_ref[...]], axis=1)
    key = lax.broadcasted_iota(jnp.int32, (HALF, SHARD), 0)
    query = lax.broadcasted_iota(jnp.int32, (HALF, SHARD), 1)
    key_place = (key // 16) * 32 + key % 16 + core * 16
    inside = query % HALF
    query_place = (inside // 16) * 32 + inside % 16 + jnp.where(query < HALF, core, 1 - core) * 16
    allowed = key_place <= query_place
    total = jnp.zeros((HD, SHARD), jnp.float32)
    for number, kv in enumerate((kv0, kv1, kv2, kv3)):
        scores = lax.dot_general(
            kv[:HD, :], q_cols, (((0,), (0,)), ((), ())), preferred_element_type=jnp.float32
        )
        weights = scores * scores
        if number == 0:
            weights = jnp.where(allowed, weights, 0.0)
        else:
            weights = jnp.where(core_ref[1] >= number, weights, 0.0)
        total = total + jnp.dot(
            kv[HD:, :], weights.astype(jnp.bfloat16), preferred_element_type=jnp.float32
        )
    upper = total[:64] + carried_ref[...]
    lower = total[64:]
    mine_ref[...] = jnp.concatenate([upper[:, :HALF], lower[:, :HALF]], axis=0).T
    send_ref[...] = jnp.concatenate([lower[:, HALF:], upper[:, HALF:]], axis=0).T.astype(jnp.bfloat16)


def window_part(core, q_own, q_other, kvs, carried):
    return pl.pallas_call(
        window_kernel,
        out_shape=(
            jax.ShapeDtypeStruct((HALF, HD), jnp.float32),
            jax.ShapeDtypeStruct((HALF, HD), jnp.bfloat16),
        ),
        in_specs=[pl.BlockSpec(memory_space=pltpu.SMEM)]
        + [pl.BlockSpec(memory_space=pltpu.VMEM)] * 7,
        out_specs=(pl.BlockSpec(memory_space=pltpu.VMEM),) * 2,
        compiler_params=pltpu.CompilerParams(vmem_limit_bytes=32 * 1024 * 1024),
        name="window",
    )(core, q_own, q_other, *kvs, carried)


def norm_kernel(core_ref, tokens_ref, gain_ref, out_ref):
    floats = tokens_ref[:, 0].astype(jnp.float32).reshape(128, D)
    out_ref[...] = norm_scaled(floats, gain_ref[...]).astype(jnp.bfloat16)


def norm_part(core, tokens, gain):
    return pl.pallas_call(
        norm_kernel,
        grid_spec=pltpu.PrefetchScalarGridSpec(
            num_scalar_prefetch=1,
            grid=(2,),
            in_specs=[
                pl.BlockSpec((8, 1, 16, D), lambda i, core: (i, core[0], 0, 0)),
                pl.BlockSpec((1, D), lambda i, core: (0, 0)),
            ],
            out_specs=pl.BlockSpec((128, D), lambda i, core: (i, 0)),
        ),
        out_shape=jax.ShapeDtypeStruct((HALF, D), jnp.bfloat16),
        compiler_params=LIMIT,
        name="norm",
    )(core, tokens.reshape(16, 2, 16, D), gain.reshape(1, D))


def project_kernel(core_ref, normed_ref, own_ref, other_ref, q_ref, kv_ref):
    core = core_ref[0]
    normed = normed_ref[...]

    def times(ref):
        return lax.dot_general(
            ref[...].reshape(192, D),
            normed,
            (((1,), (1,)), ((), ())),
            preferred_element_type=jnp.float32,
        ).astype(jnp.bfloat16)

    own, other = times(own_ref), times(other_ref)
    own_at = pl.multiple_of(core * 64, 64)
    other_at = pl.multiple_of((1 - core) * 64, 64)
    q_ref[pl.ds(own_at, 64), :] = own[:64]
    q_ref[pl.ds(other_at, 64), :] = other[:64]
    kv_ref[pl.ds(own_at, 64), :] = own[64:128]
    kv_ref[pl.ds(other_at, 64), :] = other[64:128]
    kv_ref[128:192, :] = own[128:]
    kv_ref[192:256, :] = other[128:]


def project_part(core, normed, own, other):
    return pl.pallas_call(
        project_kernel,
        out_shape=(
            jax.ShapeDtypeStruct((HD, HALF), jnp.bfloat16),
            jax.ShapeDtypeStruct((2 * HD, HALF), jnp.bfloat16),
        ),
        in_specs=[SMEM, VMEM, VMEM, VMEM],
        out_specs=(VMEM, VMEM),
        compiler_params=LIMIT,
        name="project",
    )(core, normed, own, other)


def attend_kernel(place_ref, mine_ref, received_ref, *rest):
    outs, scratch = rest[:4], rest[4]
    raw = (mine_ref[...] + received_ref[...].astype(jnp.float32)) / HD
    scratch[...] = norm_scaled(raw, 1.0).reshape(4, 64, HD)
    for step, out in enumerate(outs):
        at = pl.multiple_of(lax.rem(place_ref[1] + step, 4) * SLAB, SLAB)
        out[...] = scratch[:, pl.ds(at, SLAB), :].reshape(64, HD).astype(jnp.bfloat16)


def attend_part(place, mine, received):
    return pl.pallas_call(
        attend_kernel,
        out_shape=(jax.ShapeDtypeStruct((64, HD), jnp.bfloat16),) * 4,
        in_specs=[SMEM, VMEM, VMEM],
        out_specs=(VMEM,) * 4,
        scratch_shapes=[pltpu.VMEM((4, 64, HD), jnp.float32)],
        compiler_params=LIMIT,
        name="attend",
    )(place, mine, received)


def output_kernel(place_ref, *rest):
    pieces, own, other, outs, scratch = rest[:4], rest[4:8], rest[8:12], rest[12:16], rest[16]
    loaded = [piece[...] for piece in pieces]
    for at in range(0, D, 512):
        total = jnp.zeros((64, 512), jnp.float32)
        for step in range(4):
            total = total + jnp.dot(
                loaded[step][:, :64],
                own[step][:, at : at + 512],
                preferred_element_type=jnp.float32,
            )
            total = total + jnp.dot(
                loaded[step][:, 64:],
                other[step][:, at : at + 512],
                preferred_element_type=jnp.float32,
            )
        scratch[:, at : at + 512] = total
    for step, out in enumerate(outs):
        at = pl.multiple_of(lax.rem(place_ref[0] + step, 4) * SLAB, SLAB)
        out[...] = scratch[pl.ds(at, SLAB), :].astype(out.dtype)


def output_part(place, pieces, own, other):
    return pl.pallas_call(
        output_kernel,
        out_shape=(jax.ShapeDtypeStruct((SLAB, D), jnp.float32),)
        + (jax.ShapeDtypeStruct((SLAB, D), jnp.bfloat16),) * 3,
        in_specs=[SMEM] + [VMEM] * 12,
        out_specs=(VMEM,) * 4,
        scratch_shapes=[pltpu.VMEM((64, D), jnp.float32)],
        compiler_params=LIMIT,
        name="output",
    )(place, *pieces, *own, *other)


def map_kernel(index_ref, rows_ref, lanes_ref):
    index = index_ref[...]
    expert = lax.broadcasted_iota(jnp.int32, (SLAB, EXPERTS), 1)
    chosen = jnp.zeros((SLAB, EXPERTS), jnp.float32)
    for k in range(TOP):
        chosen = chosen + jnp.where(index[:, k : k + 1] == expert, 1.0, 0.0)
    before = lax.broadcasted_iota(jnp.int32, (SLAB, SLAB), 0) > lax.broadcasted_iota(
        jnp.int32, (SLAB, SLAB), 1
    )
    slot = jnp.dot(
        jnp.where(before, 1.0, 0.0).astype(jnp.bfloat16),
        chosen.astype(jnp.bfloat16),
        preferred_element_type=jnp.float32,
    )
    code = jnp.where(chosen > 0.5, slot, -1.0).astype(jnp.bfloat16)
    lane = lax.broadcasted_iota(jnp.int32, (SLAB, TILE_ROWS), 1)
    wide = jnp.dot(code, spread_map(), preferred_element_type=jnp.float32)
    lanes_ref[...] = jnp.where(
        wide == ((lane // PIECES) % CAP).astype(jnp.float32), 1.0, 0.0
    )
    token = lax.broadcasted_iota(jnp.int32, (SLAB, 256), 0)
    column = lax.broadcasted_iota(jnp.int32, (SLAB, 256), 1)
    by_column = lax.dot_general(
        code,
        jnp.where(column % SLAB == token, 1.0, 0.0).astype(jnp.bfloat16),
        (((0,), (0,)), ((), ())),
        preferred_element_type=jnp.float32,
    ).astype(jnp.bfloat16)
    row_expert = lax.broadcasted_iota(jnp.int32, (TILE_ROWS, EXPERTS), 0) // (CAP * PIECES)
    pick = jnp.where(
        row_expert == lax.broadcasted_iota(jnp.int32, (TILE_ROWS, EXPERTS), 1), 1.0, 0.0
    ).astype(jnp.bfloat16)
    tall = jnp.dot(pick, by_column, preferred_element_type=jnp.float32)
    row = lax.broadcasted_iota(jnp.int32, (TILE_ROWS, 256), 0)
    piece = lax.broadcasted_iota(jnp.int32, (TILE_ROWS, 256), 1) // SLAB
    rows_ref[...] = jnp.where(
        (tall == ((row // PIECES) % CAP).astype(jnp.float32)) & (row % PIECES == piece), 1.0, 0.0
    ).astype(jnp.bfloat16)


def spread_map():
    lane_expert = lax.broadcasted_iota(jnp.int32, (EXPERTS, TILE_ROWS), 1) // (CAP * PIECES)
    return jnp.where(
        lane_expert == lax.broadcasted_iota(jnp.int32, (EXPERTS, TILE_ROWS), 0), 1.0, 0.0
    ).astype(jnp.bfloat16)


def map_part(index):
    return pl.pallas_call(
        map_kernel,
        out_shape=(
            jax.ShapeDtypeStruct((TILE_ROWS, 256), jnp.bfloat16),
            jax.ShapeDtypeStruct((SLAB, TILE_ROWS), jnp.float32),
        ),
        in_specs=[VMEM],
        out_specs=(VMEM, VMEM),
        compiler_params=LIMIT,
        name="maps",
    )(index)


def dispatch_kernel(slab_ref, own_ref, r1, r2, r3, gain_ref, router_ref, rows_ref, residual_ref, out_ref, gates_ref):
    residual = slab_ref[...].astype(jnp.float32) + own_ref[...]
    for received in (r1, r2, r3):
        residual = residual + received[...].astype(jnp.float32)
    residual_ref[...] = residual
    inputs = norm_scaled(residual, gain_ref[...]).astype(jnp.bfloat16)
    logits = lax.dot_general(
        inputs, router_ref[...], (((1,), (1,)), ((), ())), preferred_element_type=jnp.float32
    )
    gates_ref[...] = jax.nn.sigmoid(logits)
    tall = jnp.concatenate([inputs[:, at : at + 128] for at in range(0, D, 128)], axis=0)
    out_ref[...] = jnp.dot(rows_ref[...], tall, preferred_element_type=jnp.float32).astype(
        jnp.bfloat16
    )


def dispatch_part(slab, own, received, gain, router, rows):
    return pl.pallas_call(
        dispatch_kernel,
        out_shape=(
            jax.ShapeDtypeStruct((SLAB, D), jnp.float32),
            jax.ShapeDtypeStruct((TILE_ROWS, 128), jnp.bfloat16),
            jax.ShapeDtypeStruct((SLAB, EXPERTS), jnp.float32),
        ),
        in_specs=[VMEM] * 8,
        out_specs=(VMEM,) * 3,
        compiler_params=LIMIT,
        name="dispatch",
    )(slab, own, *received, gain.reshape(1, D), router, rows)


def gate_kernel(gates_ref, lanes_ref, out_ref):
    wide = jnp.dot(
        gates_ref[...].astype(jnp.bfloat16), spread_map(), preferred_element_type=jnp.float32
    )
    wide = wide * lanes_ref[...]
    piece = lax.broadcasted_iota(jnp.int32, (SLAB, TILE_ROWS), 1) % PIECES
    for at in range(PIECES):
        out_ref[at * SLAB : (at + 1) * SLAB, :] = jnp.where(piece == at, wide, 0.0).astype(
            jnp.bfloat16
        )


def gate_part(gates, lanes):
    return pl.pallas_call(
        gate_kernel,
        out_shape=jax.ShapeDtypeStruct((256, TILE_ROWS), jnp.bfloat16),
        in_specs=[VMEM, VMEM],
        out_specs=VMEM,
        compiler_params=LIMIT,
        name="gates",
    )(gates, lanes)


def expert_kernel(
    rows_ref, first_own, second_own, first_other, second_other, out_ref,
    first_ref, second_ref, flat_ref, input_ref, total_ref, first_sem, second_sem,
):
    sources = ((first_own, second_own), (first_other, second_other))
    copies = []
    for piece, (first, second) in enumerate(sources):
        for part in range(2):
            copies.append(
                pltpu.make_async_copy(
                    first.at[part], first_ref.at[piece, part], first_sem.at[piece, part]
                )
            )
        copies.append(
            pltpu.make_async_copy(second, second_ref.at[piece], second_sem.at[piece])
        )
    for copy in copies:
        copy.start()
    flat_ref[...] = rows_ref[...].astype(jnp.float32)
    for at in range(PIECES):
        input_ref[:, at * 128 : (at + 1) * 128] = flat_ref[
            pl.ds(at, ROWS, stride=PIECES), :
        ].astype(jnp.bfloat16)
    for piece in range(2):
        copies[3 * piece].wait()
        gate = jnp.dot(input_ref[...], first_ref[piece, 0], preferred_element_type=jnp.float32)
        copies[3 * piece + 1].wait()
        up = jnp.dot(input_ref[...], first_ref[piece, 1], preferred_element_type=jnp.float32)
        hidden = (gate / (1.0 + jnp.exp(-gate)) * up).astype(jnp.bfloat16)
        copies[3 * piece + 2].wait()
        product = jnp.dot(hidden, second_ref[piece], preferred_element_type=jnp.float32)
        if piece == 0:
            total_ref[...] = product
        else:
            total_ref[...] += product
    for at in range(PIECES):
        flat_ref[pl.ds(at, ROWS, stride=PIECES), :] = total_ref[:, at * 128 : (at + 1) * 128]
    out_ref[...] = flat_ref[...].astype(jnp.bfloat16)


def expert_part(rows, first, second, first_other, second_other):
    anywhere = pl.BlockSpec(memory_space=pl.ANY)
    width = second.shape[0]
    return pl.pallas_call(
        expert_kernel,
        out_shape=jax.ShapeDtypeStruct((TILE_ROWS, 128), jnp.bfloat16),
        in_specs=[VMEM] + [anywhere] * 4,
        out_specs=VMEM,
        scratch_shapes=[
            pltpu.VMEM((2, 2, D, width), jnp.bfloat16),
            pltpu.VMEM((2, width, D), jnp.bfloat16),
            pltpu.VMEM((TILE_ROWS, 128), jnp.float32),
            pltpu.VMEM((ROWS, D), jnp.bfloat16),
            pltpu.VMEM((ROWS, D), jnp.float32),
            pltpu.SemaphoreType.DMA((2, 2)),
            pltpu.SemaphoreType.DMA((2,)),
        ],
        compiler_params=LIMIT,
        name="experts",
    )(rows, first, second, first_other, second_other)


def combine_kernel(residual_ref, gates_ref, rows_ref, out_ref):
    tall = jnp.dot(gates_ref[...], rows_ref[...], preferred_element_type=jnp.float32)
    for at in range(PIECES):
        columns = slice(at * 128, (at + 1) * 128)
        out_ref[:, columns] = (
            residual_ref[:, columns] + tall[at * SLAB : (at + 1) * SLAB, :]
        ).astype(jnp.bfloat16)


def combine_part(residual, gates, rows):
    return pl.pallas_call(
        combine_kernel,
        out_shape=jax.ShapeDtypeStruct((SLAB, D), jnp.bfloat16),
        in_specs=[VMEM] * 3,
        out_specs=VMEM,
        compiler_params=LIMIT,
        name="combine",
    )(residual, gates, rows)


def chips(rows):
    shaped = rows.reshape(EXPERTS, CAP * PIECES, 128)
    return lax.all_to_all(shaped, CHIP_AXES, split_axis=0, concat_axis=0, tiled=True).reshape(
        TILE_ROWS, 128
    )


def body(
    tokens,
    attention_gain,
    head_weights,
    carried_state,
    output_weight,
    expert_gain,
    router_weight,
    expert_index,
    expert_first,
    expert_second,
):
    z, y, c = (lax.axis_index(name) for name in ("z", "y", "c"))
    place = scalars(z, y, c)
    core = scalars(c)
    own_weights = head_weights.transpose(0, 2, 1)
    other_weights = swap_core(own_weights)
    normed = norm_part(core, tokens, attention_gain)
    q_own, kv = project_part(core, normed, own_weights, other_weights)
    kvs = [kv] + [shift(kv, "x", step) for step in (1, 2, 3)]
    q_other = swap_core(q_own)
    later = lax.optimization_barrier((kv, output_weight, expert_first, expert_second))[1:]
    output_own = [later[0]] + [shift(later[0], "y", step) for step in (1, 2, 3)]
    output_other = [swap_core(rows) for rows in output_own]
    first_other, second_other = swap_core(later[1]), swap_core(later[2])
    rows_map, lanes_map = map_part(expert_index)

    carried = carried_part(carried_state.T, q_own, q_other)
    x = lax.axis_index("x")
    mine, send = window_part(scalars(c, x), q_own, q_other, kvs, carried)
    pieces = attend_part(place, mine, swap_core(send))
    pieces = [pieces[0]] + [shift(pieces[step], "y", step) for step in (1, 2, 3)]
    sums = output_part(place, pieces, output_own, output_other)
    received = [shift(sums[step], "z", step) for step in (1, 2, 3)]
    slab = lax.dynamic_slice_in_dim(tokens, ((z * 4 + y) * 2 + c) * SLAB, SLAB, 0)
    residual, outgoing, gates = dispatch_part(
        slab, sums[0], received, expert_gain, router_weight.T, rows_map
    )
    arrived = chips(outgoing)
    gate_map = gate_part(gates, lanes_map)
    produced = expert_part(arrived, expert_first, expert_second, first_other, second_other)
    return combine_part(residual, gate_map, chips(produced))


def solution(mesh):
    fine = Mesh(mesh.devices.reshape(4, 4, 4, 2), ("x", "z", "y", "c"))
    head = ("z", "y", "c")
    every = ("x", "z", "y", "c")
    in_specs = (
        P("x", None),
        P(),
        P(None, None, head),
        P(None, head),
        P(head, None),
        P(),
        P(),
        P(every, None),
        P(None, None, every),
        P(every, None),
    )
    return jax.shard_map(body, mesh=fine, in_specs=in_specs, out_specs=P(every, None), check_vma=False)
```

```python
import math

import jax
import jax.numpy as jnp
from jax import lax
from jax.experimental import pallas as pl
from jax.experimental.pallas import tpu as pltpu
from jax.sharding import Mesh
from jax.sharding import PartitionSpec as P

HD = 128
D = 2048
STATE = 8256
EXPERTS = 64
TOP = 8
CAP = 3
SLAB = 16
HALF = 256
SHARD = 512
CHIP_AXES = ("x", "z", "y")


def swap_core(array):
    return lax.ppermute(array, "c", [(0, 1), (1, 0)])


def shift(array, axis, step):
    return lax.ppermute(array, axis, [(i, (i + step) % 4) for i in range(4)])


VMEM = pl.BlockSpec(memory_space=pltpu.VMEM)


def room(mebibytes):
    return pltpu.CompilerParams(vmem_limit_bytes=int(mebibytes * 1024 * 1024))


def cost(microseconds):
    return pl.CostEstimate(
        flops=int(microseconds * 1e9), bytes_accessed=int(microseconds * 3e6), transcendentals=0
    )


ROWS = EXPERTS * CAP
PIECES = D // 128
TILE_ROWS = ROWS * PIECES


def norm_scaled(values, gain):
    return values * lax.rsqrt(jnp.mean(values * values, axis=-1, keepdims=True) + 1e-06) * gain


GROUP = 8
TAIL_AT = 8064


def carried_kernel(m_ref, q_own_ref, q_other_ref, out_ref, q_ref, w_a, w_b, tail_ref):
    tail_ref[:, : STATE - TAIL_AT] = m_ref[:, TAIL_AT:]
    q_ref[:, :HALF] = q_own_ref[...].astype(jnp.float32)
    q_ref[:, HALF:] = q_other_ref[...].astype(jnp.float32)
    q_cols = jnp.concatenate([q_own_ref[...], q_other_ref[...]], axis=1)
    lane = lax.broadcasted_iota(jnp.int32, (64, 128), 1)
    root = math.sqrt(2.0)
    weights = (w_a, w_b)

    def prepare(number):
        base = number * GROUP
        for k in range(GROUP):
            i = base + k
            offset = 127 * i - (i * (i - 1)) // 2
            tile, turn = (offset // 128) * 128, offset % 128
            if tile < TAIL_AT:
                first, second = m_ref[:, tile : tile + 128], m_ref[:, tile + 128 : tile + 256]
            else:
                first, second = tail_ref[:, :128], tail_ref[:, 128:]
            if turn == 0:
                joined = first
            else:
                joined = jnp.where(
                    lane < 128 - turn,
                    pltpu.roll(first, 128 - turn, 1),
                    pltpu.roll(second, 128 - turn, 1),
                )
            weights[number % 2][64 * k : 64 * k + 64, :] = jnp.where(
                lane > i, joined * root, jnp.where(lane == i, joined, 0.0)
            ).astype(jnp.bfloat16)

    prepare(0)
    for number in range(HD // GROUP):
        spread = jnp.dot(weights[number % 2][...], q_cols, preferred_element_type=jnp.float32)
        if number + 1 < HD // GROUP:
            prepare(number + 1)
        base = number * GROUP
        total = spread[0:64] * q_ref[base : base + 1, :]
        for k in range(1, GROUP):
            total = total + spread[64 * k : 64 * k + 64] * q_ref[base + k : base + k + 1, :]
        if number == 0:
            out_ref[...] = total
        else:
            out_ref[...] += total


def carried_part(state_cols, q_own, q_other):
    return pl.pallas_call(
        carried_kernel,
        out_shape=jax.ShapeDtypeStruct((64, SHARD), jnp.float32),
        in_specs=[VMEM] * 3,
        out_specs=VMEM,
        scratch_shapes=[
            pltpu.VMEM((HD, SHARD), jnp.float32),
            pltpu.VMEM((64 * GROUP, HD), jnp.bfloat16),
            pltpu.VMEM((64 * GROUP, HD), jnp.bfloat16),
            pltpu.VMEM((64, 256), jnp.float32),
        ],
        compiler_params=room(2),
        cost_estimate=cost(5),
        name="carried",
    )(state_cols, q_own, q_other)


def window_kernel(q_own_ref, q_other_ref, kv0, kv1, kv2, kv3, carried_ref, mine_ref, send_ref):
    core, shard = lax.axis_index("c"), lax.axis_index("x")
    q_cols = jnp.concatenate([q_own_ref[...], q_other_ref[...]], axis=1)
    key = lax.broadcasted_iota(jnp.int32, (HALF, SHARD), 0)
    query = lax.broadcasted_iota(jnp.int32, (HALF, SHARD), 1)
    key_place = (key // 16) * 32 + key % 16 + core * 16
    inside = query % HALF
    query_place = (inside // 16) * 32 + inside % 16 + jnp.where(query < HALF, core, 1 - core) * 16
    allowed = key_place <= query_place
    total = jnp.zeros((HD, SHARD), jnp.float32)
    for number, kv in enumerate((kv0, kv1, kv2, kv3)):
        scores = lax.dot_general(
            kv[:HD, :], q_cols, (((0,), (0,)), ((), ())), preferred_element_type=jnp.float32
        )
        weights = scores * scores
        if number == 0:
            weights = jnp.where(allowed, weights, 0.0)
        else:
            weights = jnp.where(shard >= number, weights, 0.0)
        total = total + jnp.dot(
            kv[HD:, :], weights.astype(jnp.bfloat16), preferred_element_type=jnp.float32
        )
    upper = total[:64] + carried_ref[...]
    lower = total[64:]
    mine_ref[...] = jnp.concatenate([upper[:, :HALF], lower[:, :HALF]], axis=0).T
    send_ref[...] = jnp.concatenate([lower[:, HALF:], upper[:, HALF:]], axis=0).T.astype(jnp.bfloat16)


def window_part(q_own, q_other, kvs, carried):
    return pl.pallas_call(
        window_kernel,
        out_shape=(
            jax.ShapeDtypeStruct((HALF, HD), jnp.float32),
            jax.ShapeDtypeStruct((HALF, HD), jnp.bfloat16),
        ),
        in_specs=[VMEM] * 7,
        out_specs=(VMEM,) * 2,
        compiler_params=room(2),
        cost_estimate=cost(2),
        name="window",
    )(q_own, q_other, *kvs, carried)


def norm_kernel(tokens_ref, gain_ref, out_ref, slab_ref):
    core = lax.axis_index("c")
    slab_ref[...] = tokens_ref[lax.axis_index("z") * 4 + lax.axis_index("y"), core]
    for k in range(4):
        floats = tokens_ref[4 * k : 4 * k + 4, core].astype(jnp.float32).reshape(64, D)
        out_ref[64 * k : 64 * k + 64, :] = norm_scaled(floats, gain_ref[...]).astype(jnp.bfloat16)


def norm_part(tokens, gain):
    return pl.pallas_call(
        norm_kernel,
        out_shape=(
            jax.ShapeDtypeStruct((HALF, D), jnp.bfloat16),
            jax.ShapeDtypeStruct((SLAB, D), jnp.bfloat16),
        ),
        in_specs=[VMEM, VMEM],
        out_specs=(VMEM, VMEM),
        compiler_params=room(2),
        cost_estimate=cost(1),
        name="norm",
    )(tokens.reshape(16, 2, 16, D), gain.reshape(1, D))


def project_kernel(normed_ref, own_ref, other_ref, q_ref, kv_ref):
    core = lax.axis_index("c")
    normed = normed_ref[...]

    def times(ref):
        return lax.dot_general(
            ref[...].reshape(192, D),
            normed,
            (((1,), (1,)), ((), ())),
            preferred_element_type=jnp.float32,
        ).astype(jnp.bfloat16)

    own, other = times(own_ref), times(other_ref)
    own_at = pl.multiple_of(core * 64, 64)
    other_at = pl.multiple_of((1 - core) * 64, 64)
    q_ref[pl.ds(own_at, 64), :] = own[:64]
    q_ref[pl.ds(other_at, 64), :] = other[:64]
    kv_ref[pl.ds(own_at, 64), :] = own[64:128]
    kv_ref[pl.ds(other_at, 64), :] = other[64:128]
    kv_ref[128:192, :] = own[128:]
    kv_ref[192:256, :] = other[128:]


def project_part(normed, own, other):
    return pl.pallas_call(
        project_kernel,
        out_shape=(
            jax.ShapeDtypeStruct((HD, HALF), jnp.bfloat16),
            jax.ShapeDtypeStruct((2 * HD, HALF), jnp.bfloat16),
        ),
        in_specs=[VMEM, VMEM, VMEM],
        out_specs=(VMEM, VMEM),
        compiler_params=room(2),
        cost_estimate=cost(1),
        name="project",
    )(normed, own, other)


def attend_kernel(mine_ref, received_ref, *rest):
    outs, scratch = rest[:4], rest[4]
    raw = (mine_ref[...] + received_ref[...].astype(jnp.float32)) / HD
    scratch[...] = norm_scaled(raw, 1.0).reshape(4, 64, HD)
    for step, out in enumerate(outs):
        at = pl.multiple_of(lax.rem(lax.axis_index("y") + step, 4) * SLAB, SLAB)
        out[...] = scratch[:, pl.ds(at, SLAB), :].reshape(64, HD).astype(jnp.bfloat16)


def attend_part(mine, received):
    return pl.pallas_call(
        attend_kernel,
        out_shape=(jax.ShapeDtypeStruct((64, HD), jnp.bfloat16),) * 4,
        in_specs=[VMEM, VMEM],
        out_specs=(VMEM,) * 4,
        scratch_shapes=[pltpu.VMEM((4, 64, HD), jnp.float32)],
        compiler_params=room(2),
        cost_estimate=cost(0.7),
        name="attend",
    )(mine, received)


def pack_kernel(*refs):
    for step in range(4):
        refs[4][64 * step : 64 * step + 64, :] = refs[step][...]


def pack_part(rows):
    return pl.pallas_call(
        pack_kernel,
        out_shape=jax.ShapeDtypeStruct((HALF, D), jnp.bfloat16),
        in_specs=[VMEM] * 4,
        out_specs=VMEM,
        compiler_params=room(2),
        cost_estimate=cost(0.5),
        name="pack",
    )(*rows)


def output_kernel(*rest):
    pieces, own, other, outs, scratch = rest[:4], rest[4], rest[5], rest[6:10], rest[10]
    loaded = [piece[...] for piece in pieces]
    for at in range(0, D, 512):
        total = jnp.zeros((64, 512), jnp.float32)
        for step in range(4):
            total = total + jnp.dot(
                loaded[step][:, :64],
                own[64 * step : 64 * step + 64, at : at + 512],
                preferred_element_type=jnp.float32,
            )
            total = total + jnp.dot(
                loaded[step][:, 64:],
                other[64 * step : 64 * step + 64, at : at + 512],
                preferred_element_type=jnp.float32,
            )
        scratch[:, at : at + 512] = total
    for step, out in enumerate(outs):
        at = pl.multiple_of(lax.rem(lax.axis_index("z") + step, 4) * SLAB, SLAB)
        out[...] = scratch[pl.ds(at, SLAB), :].astype(out.dtype)


def output_part(pieces, own, other):
    return pl.pallas_call(
        output_kernel,
        out_shape=(jax.ShapeDtypeStruct((SLAB, D), jnp.float32),)
        + (jax.ShapeDtypeStruct((SLAB, D), jnp.bfloat16),) * 3,
        in_specs=[VMEM] * 6,
        out_specs=(VMEM,) * 4,
        scratch_shapes=[pltpu.VMEM((64, D), jnp.float32)],
        compiler_params=room(2),
        cost_estimate=cost(2),
        name="output",
    )(*pieces, own, other)


def map_kernel(index_ref, gain_ref, rows_ref, lanes_ref, gain_out):
    gain_out[...] = gain_ref[...]
    index = index_ref[...]
    expert = lax.broadcasted_iota(jnp.int32, (EXPERTS, SLAB), 0)
    chosen = jnp.zeros((EXPERTS, SLAB), jnp.float32)
    for k in range(TOP):
        chosen = chosen + jnp.where(index[k : k + 1, :] == expert, 1.0, 0.0)
    before = lax.broadcasted_iota(jnp.int32, (SLAB, SLAB), 0) < lax.broadcasted_iota(
        jnp.int32, (SLAB, SLAB), 1
    )
    slot = jnp.dot(
        chosen.astype(jnp.bfloat16),
        jnp.where(before, 1.0, 0.0).astype(jnp.bfloat16),
        preferred_element_type=jnp.float32,
    )
    code = jnp.where(chosen > 0.5, slot, -1.0).astype(jnp.bfloat16)
    lane = lax.broadcasted_iota(jnp.int32, (SLAB, TILE_ROWS), 1)
    wide = lax.dot_general(
        code, spread_map(), (((0,), (0,)), ((), ())), preferred_element_type=jnp.float32
    )
    lanes_ref[...] = jnp.where(
        wide == ((lane // PIECES) % CAP).astype(jnp.float32), 1.0, 0.0
    )
    token = lax.broadcasted_iota(jnp.int32, (SLAB, 256), 0)
    column = lax.broadcasted_iota(jnp.int32, (SLAB, 256), 1)
    by_column = jnp.dot(
        code,
        jnp.where(column % SLAB == token, 1.0, 0.0).astype(jnp.bfloat16),
        preferred_element_type=jnp.float32,
    ).astype(jnp.bfloat16)
    row_expert = lax.broadcasted_iota(jnp.int32, (TILE_ROWS, EXPERTS), 0) // (CAP * PIECES)
    pick = jnp.where(
        row_expert == lax.broadcasted_iota(jnp.int32, (TILE_ROWS, EXPERTS), 1), 1.0, 0.0
    ).astype(jnp.bfloat16)
    tall = jnp.dot(pick, by_column, preferred_element_type=jnp.float32)
    row = lax.broadcasted_iota(jnp.int32, (TILE_ROWS, 256), 0)
    piece = lax.broadcasted_iota(jnp.int32, (TILE_ROWS, 256), 1) // SLAB
    rows_ref[...] = jnp.where(
        (tall == ((row // PIECES) % CAP).astype(jnp.float32)) & (row % PIECES == piece), 1.0, 0.0
    ).astype(jnp.bfloat16)


def spread_map():
    lane_expert = lax.broadcasted_iota(jnp.int32, (EXPERTS, TILE_ROWS), 1) // (CAP * PIECES)
    return jnp.where(
        lane_expert == lax.broadcasted_iota(jnp.int32, (EXPERTS, TILE_ROWS), 0), 1.0, 0.0
    ).astype(jnp.bfloat16)


def map_part(index, gain):
    return pl.pallas_call(
        map_kernel,
        out_shape=(
            jax.ShapeDtypeStruct((TILE_ROWS, 256), jnp.bfloat16),
            jax.ShapeDtypeStruct((SLAB, TILE_ROWS), jnp.float32),
            jax.ShapeDtypeStruct((1, D), jnp.float32),
        ),
        in_specs=[VMEM, VMEM],
        out_specs=(VMEM,) * 3,
        compiler_params=room(14),
        cost_estimate=cost(2),
        name="maps",
    )(index, gain.reshape(1, D))


def dispatch_kernel(slab_ref, own_ref, r1, r2, r3, gain_ref, router_ref, rows_ref, residual_ref, out_ref, gates_ref):
    residual = slab_ref[...].astype(jnp.float32) + own_ref[...]
    for received in (r1, r2, r3):
        residual = residual + received[...].astype(jnp.float32)
    residual_ref[...] = residual
    inputs = norm_scaled(residual, gain_ref[...]).astype(jnp.bfloat16)
    logits = lax.dot_general(
        inputs, router_ref[...], (((1,), (1,)), ((), ())), preferred_element_type=jnp.float32
    )
    gates_ref[...] = jax.nn.sigmoid(logits)
    tall = jnp.concatenate([inputs[:, at : at + 128] for at in range(0, D, 128)], axis=0)
    out_ref[...] = jnp.dot(rows_ref[...], tall, preferred_element_type=jnp.float32).astype(
        jnp.bfloat16
    )


def dispatch_part(slab, own, received, gain, router, rows):
    return pl.pallas_call(
        dispatch_kernel,
        out_shape=(
            jax.ShapeDtypeStruct((SLAB, D), jnp.float32),
            jax.ShapeDtypeStruct((TILE_ROWS, 128), jnp.bfloat16),
            jax.ShapeDtypeStruct((SLAB, EXPERTS), jnp.float32),
        ),
        in_specs=[VMEM] * 8,
        out_specs=(VMEM,) * 3,
        compiler_params=room(6),
        cost_estimate=cost(1),
        name="dispatch",
    )(slab, own, *received, gain, router, rows)


def gate_kernel(gates_ref, lanes_ref, out_ref):
    wide = jnp.dot(
        gates_ref[...].astype(jnp.bfloat16), spread_map(), preferred_element_type=jnp.float32
    )
    wide = wide * lanes_ref[...]
    piece = lax.broadcasted_iota(jnp.int32, (SLAB, TILE_ROWS), 1) % PIECES
    for at in range(PIECES):
        out_ref[at * SLAB : (at + 1) * SLAB, :] = jnp.where(piece == at, wide, 0.0).astype(
            jnp.bfloat16
        )


def gate_part(gates, lanes):
    return pl.pallas_call(
        gate_kernel,
        out_shape=jax.ShapeDtypeStruct((256, TILE_ROWS), jnp.bfloat16),
        in_specs=[VMEM, VMEM],
        out_specs=VMEM,
        compiler_params=room(8),
        cost_estimate=cost(0.5),
        name="gates",
    )(gates, lanes)


def expert_kernel(
    rows_ref, first_own, second_own, first_other, second_other, out_ref,
    first_ref, second_ref, flat_ref, input_ref, total_ref, first_sem, second_sem,
):
    sources = ((first_own, second_own), (first_other, second_other))
    copies = []
    for piece, (first, second) in enumerate(sources):
        for part in range(2):
            copies.append(
                pltpu.make_async_copy(
                    first.at[part], first_ref.at[piece, part], first_sem.at[piece, part]
                )
            )
        copies.append(
            pltpu.make_async_copy(second, second_ref.at[piece], second_sem.at[piece])
        )
    for copy in copies:
        copy.start()
    flat_ref[...] = rows_ref[...].astype(jnp.float32)
    for at in range(PIECES):
        input_ref[:, at * 128 : (at + 1) * 128] = flat_ref[
            pl.ds(at, ROWS, stride=PIECES), :
        ].astype(jnp.bfloat16)
    for piece in range(2):
        copies[3 * piece].wait()
        gate = jnp.dot(input_ref[...], first_ref[piece, 0], preferred_element_type=jnp.float32)
        copies[3 * piece + 1].wait()
        up = jnp.dot(input_ref[...], first_ref[piece, 1], preferred_element_type=jnp.float32)
        hidden = (gate / (1.0 + jnp.exp(-gate)) * up).astype(jnp.bfloat16)
        copies[3 * piece + 2].wait()
        product = jnp.dot(hidden, second_ref[piece], preferred_element_type=jnp.float32)
        if piece == 0:
            total_ref[...] = product
        else:
            total_ref[...] += product
    for at in range(PIECES):
        flat_ref[pl.ds(at, ROWS, stride=PIECES), :] = total_ref[:, at * 128 : (at + 1) * 128]
    out_ref[...] = flat_ref[...].astype(jnp.bfloat16)


def expert_part(rows, first, second, first_other, second_other):
    anywhere = pl.BlockSpec(memory_space=pl.ANY)
    width = second.shape[0]
    return pl.pallas_call(
        expert_kernel,
        out_shape=jax.ShapeDtypeStruct((TILE_ROWS, 128), jnp.bfloat16),
        in_specs=[VMEM] + [anywhere] * 4,
        out_specs=VMEM,
        scratch_shapes=[
            pltpu.VMEM((2, 2, D, width), jnp.bfloat16),
            pltpu.VMEM((2, width, D), jnp.bfloat16),
            pltpu.VMEM((TILE_ROWS, 128), jnp.float32),
            pltpu.VMEM((ROWS, D), jnp.bfloat16),
            pltpu.VMEM((ROWS, D), jnp.float32),
            pltpu.SemaphoreType.DMA((2, 2)),
            pltpu.SemaphoreType.DMA((2,)),
        ],
        compiler_params=room(24),
        cost_estimate=cost(6),
        name="experts",
    )(rows, first, second, first_other, second_other)


def combine_kernel(residual_ref, gates_ref, rows_ref, out_ref):
    tall = jnp.dot(gates_ref[...], rows_ref[...], preferred_element_type=jnp.float32)
    for at in range(PIECES):
        columns = slice(at * 128, (at + 1) * 128)
        out_ref[:, columns] = (
            residual_ref[:, columns] + tall[at * SLAB : (at + 1) * SLAB, :]
        ).astype(jnp.bfloat16)


def combine_part(residual, gates, rows):
    return pl.pallas_call(
        combine_kernel,
        out_shape=jax.ShapeDtypeStruct((SLAB, D), jnp.bfloat16),
        in_specs=[VMEM] * 3,
        out_specs=VMEM,
        compiler_params=room(4),
        cost_estimate=cost(1),
        name="combine",
    )(residual, gates, rows)


def chips(rows):
    shaped = rows.reshape(EXPERTS, CAP * PIECES, 128)
    return lax.all_to_all(shaped, CHIP_AXES, split_axis=0, concat_axis=0, tiled=True).reshape(
        TILE_ROWS, 128
    )


def body(
    tokens,
    attention_gain,
    head_weights,
    carried_state,
    output_weight,
    expert_gain,
    router_weight,
    expert_index,
    expert_first,
    expert_second,
):
    own_weights = head_weights.transpose(0, 2, 1)
    other_weights = swap_core(own_weights)
    output_own = [output_weight] + [shift(output_weight, "y", step) for step in (1, 2, 3)]
    normed, slab = norm_part(tokens, attention_gain)
    q_own, kv = project_part(normed, own_weights, other_weights)
    kvs = [kv] + [shift(kv, "x", step) for step in (1, 2, 3)]
    q_other = swap_core(q_own)
    rows_map, lanes_map, gain = map_part(expert_index.T, expert_gain)

    carried = carried_part(carried_state.T, q_own, q_other)
    mine, send = window_part(q_own, q_other, kvs, carried)
    tied = lax.optimization_barrier((swap_core(send), *output_own))
    received, output_own = tied[0], pack_part(tied[1:])
    output_other = swap_core(output_own)
    pieces = attend_part(mine, received)
    pieces = [pieces[0]] + [shift(pieces[step], "y", step) for step in (1, 2, 3)]
    sums = output_part(pieces, output_own, output_other)
    tied = lax.optimization_barrier((*sums, expert_first, expert_second))
    sums, first_given, second_given = tied[:4], tied[4], tied[5]
    first_other, second_other = swap_core(first_given), swap_core(second_given)
    summed = [shift(sums[step], "z", step) for step in (1, 2, 3)]
    residual, outgoing, gates = dispatch_part(
        slab, sums[0], summed, gain, router_weight.T, rows_map
    )
    arrived = chips(outgoing)
    gate_map = gate_part(gates, lanes_map)
    produced = expert_part(arrived, expert_first, expert_second, first_other, second_other)
    return combine_part(residual, gate_map, chips(produced))


def solution(mesh):
    fine = Mesh(mesh.devices.reshape(4, 4, 4, 2), ("x", "z", "y", "c"))
    head = ("z", "y", "c")
    every = ("x", "z", "y", "c")
    in_specs = (
        P("x", None),
        P(),
        P(None, None, head),
        P(None, head),
        P(head, None),
        P(),
        P(),
        P(every, None),
        P(None, None, every),
        P(every, None),
    )
    return jax.shard_map(body, mesh=fine, in_specs=in_specs, out_specs=P(every, None), check_vma=False)
```

```python
import math

import jax
import jax.numpy as jnp
from jax import lax
from jax.experimental import pallas as pl
from jax.experimental.pallas import tpu as pltpu
from jax.sharding import Mesh
from jax.sharding import PartitionSpec as P

HD = 128
D = 2048
STATE = 8256
EXPERTS = 64
TOP = 8
CAP = 3
SLAB = 16
HALF = 256
SHARD = 512
CHIP_AXES = ("x", "z", "y")


def swap_core(array):
    return lax.ppermute(array, "c", [(0, 1), (1, 0)])


def shift(array, axis, step):
    return lax.ppermute(array, axis, [(i, (i + step) % 4) for i in range(4)])


VMEM = pl.BlockSpec(memory_space=pltpu.VMEM)


def room(mebibytes):
    return pltpu.CompilerParams(vmem_limit_bytes=int(mebibytes * 1024 * 1024))


def cost(microseconds):
    return pl.CostEstimate(
        flops=int(microseconds * 1e9), bytes_accessed=int(microseconds * 3e6), transcendentals=0
    )


ROWS = EXPERTS * CAP
PIECES = D // 128
TILE_ROWS = ROWS * PIECES


def norm_scaled(values, gain):
    return values * lax.rsqrt(jnp.mean(values * values, axis=-1, keepdims=True) + 1e-06) * gain


GROUP = 8
TAIL_AT = 8064


def carried_kernel(m_ref, q_own_ref, q_other_ref, out_ref, q_ref, w_a, w_b, tail_ref):
    tail_ref[:, : STATE - TAIL_AT] = m_ref[:, TAIL_AT:]
    q_ref[:, :HALF] = q_own_ref[...].astype(jnp.float32)
    q_ref[:, HALF:] = q_other_ref[...].astype(jnp.float32)
    q_cols = jnp.concatenate([q_own_ref[...], q_other_ref[...]], axis=1)
    lane = lax.broadcasted_iota(jnp.int32, (64, 128), 1)
    root = math.sqrt(2.0)
    weights = (w_a, w_b)

    def prepare(number):
        base = number * GROUP
        for k in range(GROUP):
            i = base + k
            offset = 127 * i - (i * (i - 1)) // 2
            tile, turn = (offset // 128) * 128, offset % 128
            if tile < TAIL_AT:
                first, second = m_ref[:, tile : tile + 128], m_ref[:, tile + 128 : tile + 256]
            else:
                first, second = tail_ref[:, :128], tail_ref[:, 128:]
            if turn == 0:
                joined = first
            else:
                joined = jnp.where(
                    lane < 128 - turn,
                    pltpu.roll(first, 128 - turn, 1),
                    pltpu.roll(second, 128 - turn, 1),
                )
            weights[number % 2][64 * k : 64 * k + 64, :] = jnp.where(
                lane > i, joined * root, jnp.where(lane == i, joined, 0.0)
            ).astype(jnp.bfloat16)

    prepare(0)
    for number in range(HD // GROUP):
        spread = jnp.dot(weights[number % 2][...], q_cols, preferred_element_type=jnp.float32)
        if number + 1 < HD // GROUP:
            prepare(number + 1)
        base = number * GROUP
        total = spread[0:64] * q_ref[base : base + 1, :]
        for k in range(1, GROUP):
            total = total + spread[64 * k : 64 * k + 64] * q_ref[base + k : base + k + 1, :]
        if number == 0:
            out_ref[...] = total
        else:
            out_ref[...] += total


def carried_part(state_cols, q_own, q_other):
    return pl.pallas_call(
        carried_kernel,
        out_shape=jax.ShapeDtypeStruct((64, SHARD), jnp.float32),
        in_specs=[VMEM] * 3,
        out_specs=VMEM,
        scratch_shapes=[
            pltpu.VMEM((HD, SHARD), jnp.float32),
            pltpu.VMEM((64 * GROUP, HD), jnp.bfloat16),
            pltpu.VMEM((64 * GROUP, HD), jnp.bfloat16),
            pltpu.VMEM((64, 256), jnp.float32),
        ],
        compiler_params=room(2),
        cost_estimate=cost(5),
        name="carried",
    )(state_cols, q_own, q_other)


def window_kernel(q_own_ref, q_other_ref, kv0, kv1, kv2, kv3, carried_ref, mine_ref, send_ref):
    core, shard = lax.axis_index("c"), lax.axis_index("x")
    q_cols = jnp.concatenate([q_own_ref[...], q_other_ref[...]], axis=1)
    key = lax.broadcasted_iota(jnp.int32, (HALF, SHARD), 0)
    query = lax.broadcasted_iota(jnp.int32, (HALF, SHARD), 1)
    key_place = (key // 16) * 32 + key % 16 + core * 16
    inside = query % HALF
    query_place = (inside // 16) * 32 + inside % 16 + jnp.where(query < HALF, core, 1 - core) * 16
    allowed = key_place <= query_place
    total = jnp.zeros((HD, SHARD), jnp.float32)
    for number, kv in enumerate((kv0, kv1, kv2, kv3)):
        scores = lax.dot_general(
            kv[:HD, :], q_cols, (((0,), (0,)), ((), ())), preferred_element_type=jnp.float32
        )
        weights = scores * scores
        if number == 0:
            weights = jnp.where(allowed, weights, 0.0)
        else:
            weights = jnp.where(shard >= number, weights, 0.0)
        total = total + jnp.dot(
            kv[HD:, :], weights.astype(jnp.bfloat16), preferred_element_type=jnp.float32
        )
    upper = total[:64] + carried_ref[...]
    lower = total[64:]
    mine_ref[...] = jnp.concatenate([upper[:, :HALF], lower[:, :HALF]], axis=0).T
    send_ref[...] = jnp.concatenate([lower[:, HALF:], upper[:, HALF:]], axis=0).T.astype(jnp.bfloat16)


def window_part(q_own, q_other, kvs, carried):
    return pl.pallas_call(
        window_kernel,
        out_shape=(
            jax.ShapeDtypeStruct((HALF, HD), jnp.float32),
            jax.ShapeDtypeStruct((HALF, HD), jnp.bfloat16),
        ),
        in_specs=[VMEM] * 7,
        out_specs=(VMEM,) * 2,
        compiler_params=room(2),
        cost_estimate=cost(2),
        name="window",
    )(q_own, q_other, *kvs, carried)


def norm_kernel(tokens_ref, gain_ref, out_ref, slab_ref):
    core = lax.axis_index("c")
    slab_ref[...] = tokens_ref[lax.axis_index("z") * 4 + lax.axis_index("y"), core]
    for k in range(4):
        floats = tokens_ref[4 * k : 4 * k + 4, core].astype(jnp.float32).reshape(64, D)
        out_ref[64 * k : 64 * k + 64, :] = norm_scaled(floats, gain_ref[...]).astype(jnp.bfloat16)


def norm_part(tokens, gain):
    return pl.pallas_call(
        norm_kernel,
        out_shape=(
            jax.ShapeDtypeStruct((HALF, D), jnp.bfloat16),
            jax.ShapeDtypeStruct((SLAB, D), jnp.bfloat16),
        ),
        in_specs=[VMEM, VMEM],
        out_specs=(VMEM, VMEM),
        compiler_params=room(2),
        cost_estimate=cost(1),
        name="norm",
    )(tokens.reshape(16, 2, 16, D), gain.reshape(1, D))


def project_kernel(normed_ref, own_ref, other_ref, q_ref, kv_ref):
    core = lax.axis_index("c")
    normed = normed_ref[...]

    def times(ref):
        return lax.dot_general(
            ref[...].reshape(192, D),
            normed,
            (((1,), (1,)), ((), ())),
            preferred_element_type=jnp.float32,
        ).astype(jnp.bfloat16)

    own, other = times(own_ref), times(other_ref)
    own_at = pl.multiple_of(core * 64, 64)
    other_at = pl.multiple_of((1 - core) * 64, 64)
    q_ref[pl.ds(own_at, 64), :] = own[:64]
    q_ref[pl.ds(other_at, 64), :] = other[:64]
    kv_ref[pl.ds(own_at, 64), :] = own[64:128]
    kv_ref[pl.ds(other_at, 64), :] = other[64:128]
    kv_ref[128:192, :] = own[128:]
    kv_ref[192:256, :] = other[128:]


def project_part(normed, own, other):
    return pl.pallas_call(
        project_kernel,
        out_shape=(
            jax.ShapeDtypeStruct((HD, HALF), jnp.bfloat16),
            jax.ShapeDtypeStruct((2 * HD, HALF), jnp.bfloat16),
        ),
        in_specs=[VMEM, VMEM, VMEM],
        out_specs=(VMEM, VMEM),
        compiler_params=room(2),
        cost_estimate=cost(1),
        name="project",
    )(normed, own, other)


def attend_kernel(mine_ref, received_ref, *rest):
    outs, scratch = rest[:4], rest[4]
    raw = (mine_ref[...] + received_ref[...].astype(jnp.float32)) / HD
    scratch[...] = norm_scaled(raw, 1.0).reshape(4, 64, HD)
    for step, out in enumerate(outs):
        at = pl.multiple_of(lax.rem(lax.axis_index("y") + step, 4) * SLAB, SLAB)
        out[...] = scratch[:, pl.ds(at, SLAB), :].reshape(64, HD).astype(jnp.bfloat16)


def attend_part(mine, received):
    return pl.pallas_call(
        attend_kernel,
        out_shape=(jax.ShapeDtypeStruct((64, HD), jnp.bfloat16),) * 4,
        in_specs=[VMEM, VMEM],
        out_specs=(VMEM,) * 4,
        scratch_shapes=[pltpu.VMEM((4, 64, HD), jnp.float32)],
        compiler_params=room(2),
        cost_estimate=cost(0.7),
        name="attend",
    )(mine, received)


def pack_kernel(*refs):
    for step in range(4):
        refs[4][64 * step : 64 * step + 64, :] = refs[step][...]


def pack_part(rows):
    return pl.pallas_call(
        pack_kernel,
        out_shape=jax.ShapeDtypeStruct((HALF, D), jnp.bfloat16),
        in_specs=[VMEM] * 4,
        out_specs=VMEM,
        compiler_params=room(2),
        cost_estimate=cost(0.5),
        name="pack",
    )(*rows)


def output_kernel(*rest):
    pieces, own, other, outs, scratch = rest[:4], rest[4], rest[5], rest[6:10], rest[10]
    loaded = [piece[...] for piece in pieces]
    for at in range(0, D, 512):
        total = jnp.zeros((64, 512), jnp.float32)
        for step in range(4):
            total = total + jnp.dot(
                loaded[step][:, :64],
                own[64 * step : 64 * step + 64, at : at + 512],
                preferred_element_type=jnp.float32,
            )
            total = total + jnp.dot(
                loaded[step][:, 64:],
                other[64 * step : 64 * step + 64, at : at + 512],
                preferred_element_type=jnp.float32,
            )
        scratch[:, at : at + 512] = total
    for step, out in enumerate(outs):
        at = pl.multiple_of(lax.rem(lax.axis_index("z") + step, 4) * SLAB, SLAB)
        out[...] = scratch[pl.ds(at, SLAB), :].astype(out.dtype)


def output_part(pieces, own, other):
    return pl.pallas_call(
        output_kernel,
        out_shape=(jax.ShapeDtypeStruct((SLAB, D), jnp.float32),)
        + (jax.ShapeDtypeStruct((SLAB, D), jnp.bfloat16),) * 3,
        in_specs=[VMEM] * 6,
        out_specs=(VMEM,) * 4,
        scratch_shapes=[pltpu.VMEM((64, D), jnp.float32)],
        compiler_params=room(2),
        cost_estimate=cost(2),
        name="output",
    )(*pieces, own, other)


def map_kernel(index_ref, gain_ref, rows_ref, lanes_ref, gain_out):
    gain_out[...] = gain_ref[...]
    index = index_ref[...]
    expert = lax.broadcasted_iota(jnp.int32, (EXPERTS, SLAB), 0)
    chosen = jnp.zeros((EXPERTS, SLAB), jnp.float32)
    for k in range(TOP):
        chosen = chosen + jnp.where(index[k : k + 1, :] == expert, 1.0, 0.0)
    before = lax.broadcasted_iota(jnp.int32, (SLAB, SLAB), 0) < lax.broadcasted_iota(
        jnp.int32, (SLAB, SLAB), 1
    )
    slot = jnp.dot(
        chosen.astype(jnp.bfloat16),
        jnp.where(before, 1.0, 0.0).astype(jnp.bfloat16),
        preferred_element_type=jnp.float32,
    )
    code = jnp.where(chosen > 0.5, slot, -1.0).astype(jnp.bfloat16)
    lane = lax.broadcasted_iota(jnp.int32, (SLAB, TILE_ROWS), 1)
    wide = lax.dot_general(
        code, spread_map(), (((0,), (0,)), ((), ())), preferred_element_type=jnp.float32
    )
    lanes_ref[...] = jnp.where(
        wide == ((lane // PIECES) % CAP).astype(jnp.float32), 1.0, 0.0
    )
    token = lax.broadcasted_iota(jnp.int32, (SLAB, 256), 0)
    column = lax.broadcasted_iota(jnp.int32, (SLAB, 256), 1)
    by_column = jnp.dot(
        code,
        jnp.where(column % SLAB == token, 1.0, 0.0).astype(jnp.bfloat16),
        preferred_element_type=jnp.float32,
    ).astype(jnp.bfloat16)
    row_expert = lax.broadcasted_iota(jnp.int32, (TILE_ROWS, EXPERTS), 0) // (CAP * PIECES)
    pick = jnp.where(
        row_expert == lax.broadcasted_iota(jnp.int32, (TILE_ROWS, EXPERTS), 1), 1.0, 0.0
    ).astype(jnp.bfloat16)
    tall = jnp.dot(pick, by_column, preferred_element_type=jnp.float32)
    row = lax.broadcasted_iota(jnp.int32, (TILE_ROWS, 256), 0)
    piece = lax.broadcasted_iota(jnp.int32, (TILE_ROWS, 256), 1) // SLAB
    rows_ref[...] = jnp.where(
        (tall == ((row // PIECES) % CAP).astype(jnp.float32)) & (row % PIECES == piece), 1.0, 0.0
    ).astype(jnp.bfloat16)


def spread_map():
    lane_expert = lax.broadcasted_iota(jnp.int32, (EXPERTS, TILE_ROWS), 1) // (CAP * PIECES)
    return jnp.where(
        lane_expert == lax.broadcasted_iota(jnp.int32, (EXPERTS, TILE_ROWS), 0), 1.0, 0.0
    ).astype(jnp.bfloat16)


def map_part(index, gain):
    return pl.pallas_call(
        map_kernel,
        out_shape=(
            jax.ShapeDtypeStruct((TILE_ROWS, 256), jnp.bfloat16),
            jax.ShapeDtypeStruct((SLAB, TILE_ROWS), jnp.float32),
            jax.ShapeDtypeStruct((1, D), jnp.float32),
        ),
        in_specs=[VMEM, VMEM],
        out_specs=(VMEM,) * 3,
        compiler_params=room(14),
        cost_estimate=cost(2),
        name="maps",
    )(index, gain.reshape(1, D))


def dispatch_kernel(slab_ref, own_ref, r1, r2, r3, gain_ref, router_ref, rows_ref, residual_ref, out_ref, gates_ref):
    residual = slab_ref[...].astype(jnp.float32) + own_ref[...]
    for received in (r1, r2, r3):
        residual = residual + received[...].astype(jnp.float32)
    residual_ref[...] = residual
    inputs = norm_scaled(residual, gain_ref[...]).astype(jnp.bfloat16)
    logits = lax.dot_general(
        inputs, router_ref[...], (((1,), (1,)), ((), ())), preferred_element_type=jnp.float32
    )
    gates_ref[...] = jax.nn.sigmoid(logits)
    tall = jnp.concatenate([inputs[:, at : at + 128] for at in range(0, D, 128)], axis=0)
    out_ref[...] = jnp.dot(rows_ref[...], tall, preferred_element_type=jnp.float32).astype(
        jnp.bfloat16
    )


def dispatch_part(slab, own, received, gain, router, rows):
    return pl.pallas_call(
        dispatch_kernel,
        out_shape=(
            jax.ShapeDtypeStruct((SLAB, D), jnp.float32),
            jax.ShapeDtypeStruct((TILE_ROWS, 128), jnp.bfloat16),
            jax.ShapeDtypeStruct((SLAB, EXPERTS), jnp.float32),
        ),
        in_specs=[VMEM] * 8,
        out_specs=(VMEM,) * 3,
        compiler_params=room(6),
        cost_estimate=cost(1),
        name="dispatch",
    )(slab, own, *received, gain, router, rows)


def gate_kernel(gates_ref, lanes_ref, out_ref):
    wide = jnp.dot(
        gates_ref[...].astype(jnp.bfloat16), spread_map(), preferred_element_type=jnp.float32
    )
    wide = wide * lanes_ref[...]
    piece = lax.broadcasted_iota(jnp.int32, (SLAB, TILE_ROWS), 1) % PIECES
    for at in range(PIECES):
        out_ref[at * SLAB : (at + 1) * SLAB, :] = jnp.where(piece == at, wide, 0.0).astype(
            jnp.bfloat16
        )


def gate_part(gates, lanes):
    return pl.pallas_call(
        gate_kernel,
        out_shape=jax.ShapeDtypeStruct((256, TILE_ROWS), jnp.bfloat16),
        in_specs=[VMEM, VMEM],
        out_specs=VMEM,
        compiler_params=room(8),
        cost_estimate=cost(0.5),
        name="gates",
    )(gates, lanes)


def expert_kernel(
    rows_ref, first_own, second_own, first_other, second_other, out_ref, flat_ref, input_ref, total_ref
):
    flat_ref[...] = rows_ref[...].astype(jnp.float32)
    for at in range(PIECES):
        input_ref[:, at * 128 : (at + 1) * 128] = flat_ref[
            pl.ds(at, ROWS, stride=PIECES), :
        ].astype(jnp.bfloat16)
    for piece, (first, second) in enumerate(
        ((first_own, second_own), (first_other, second_other))
    ):
        gate = jnp.dot(input_ref[...], first[0], preferred_element_type=jnp.float32)
        up = jnp.dot(input_ref[...], first[1], preferred_element_type=jnp.float32)
        hidden = (gate / (1.0 + jnp.exp(-gate)) * up).astype(jnp.bfloat16)
        product = jnp.dot(hidden, second[...], preferred_element_type=jnp.float32)
        if piece == 0:
            total_ref[...] = product
        else:
            product = product + total_ref[...]
            for at in range(PIECES):
                flat_ref[pl.ds(at, ROWS, stride=PIECES), :] = product[:, at * 128 : (at + 1) * 128]
    out_ref[...] = flat_ref[...].astype(jnp.bfloat16)


def expert_part(rows, first, second, first_other, second_other):
    return pl.pallas_call(
        expert_kernel,
        out_shape=jax.ShapeDtypeStruct((TILE_ROWS, 128), jnp.bfloat16),
        in_specs=[VMEM] * 5,
        out_specs=VMEM,
        scratch_shapes=[
            pltpu.VMEM((TILE_ROWS, 128), jnp.float32),
            pltpu.VMEM((ROWS, D), jnp.bfloat16),
            pltpu.VMEM((ROWS, D), jnp.float32),
        ],
        compiler_params=room(28),
        cost_estimate=cost(5),
        name="experts",
    )(rows, first, second, first_other, second_other)


def combine_kernel(residual_ref, gates_ref, rows_ref, out_ref):
    tall = jnp.dot(gates_ref[...], rows_ref[...], preferred_element_type=jnp.float32)
    for at in range(PIECES):
        columns = slice(at * 128, (at + 1) * 128)
        out_ref[:, columns] = (
            residual_ref[:, columns] + tall[at * SLAB : (at + 1) * SLAB, :]
        ).astype(jnp.bfloat16)


def combine_part(residual, gates, rows):
    return pl.pallas_call(
        combine_kernel,
        out_shape=jax.ShapeDtypeStruct((SLAB, D), jnp.bfloat16),
        in_specs=[VMEM] * 3,
        out_specs=VMEM,
        compiler_params=room(4),
        cost_estimate=cost(1),
        name="combine",
    )(residual, gates, rows)


def chips(rows):
    shaped = rows.reshape(EXPERTS, CAP * PIECES, 128)
    return lax.all_to_all(shaped, CHIP_AXES, split_axis=0, concat_axis=0, tiled=True).reshape(
        TILE_ROWS, 128
    )


def body(
    tokens,
    attention_gain,
    head_weights,
    carried_state,
    output_weight,
    expert_gain,
    router_weight,
    expert_index,
    expert_first,
    expert_second,
):
    own_weights = head_weights.transpose(0, 2, 1)
    other_weights = swap_core(own_weights)
    output_own = [output_weight] + [shift(output_weight, "y", step) for step in (1, 2, 3)]
    normed, slab = norm_part(tokens, attention_gain)
    q_own, kv = project_part(normed, own_weights, other_weights)
    kvs = [kv] + [shift(kv, "x", step) for step in (1, 2, 3)]
    q_other = swap_core(q_own)
    rows_map, lanes_map, gain = map_part(expert_index.T, expert_gain)

    carried = carried_part(carried_state.T, q_own, q_other)
    mine, send = window_part(q_own, q_other, kvs, carried)
    tied = lax.optimization_barrier((swap_core(send), expert_first, expert_second, *output_own))
    received, output_own = tied[0], pack_part(tied[3:])
    first_other, second_other = swap_core(tied[1]), swap_core(tied[2])
    output_other = swap_core(output_own)
    pieces = attend_part(mine, received)
    pieces = [pieces[0]] + [shift(pieces[step], "y", step) for step in (1, 2, 3)]
    sums = output_part(pieces, output_own, output_other)
    summed = [shift(sums[step], "z", step) for step in (1, 2, 3)]
    residual, outgoing, gates = dispatch_part(
        slab, sums[0], summed, gain, router_weight.T, rows_map
    )
    arrived = chips(outgoing)
    gate_map = gate_part(gates, lanes_map)
    produced = expert_part(arrived, expert_first, expert_second, first_other, second_other)
    return combine_part(residual, gate_map, chips(produced))


def solution(mesh):
    fine = Mesh(mesh.devices.reshape(4, 4, 4, 2), ("x", "z", "y", "c"))
    head = ("z", "y", "c")
    every = ("x", "z", "y", "c")
    in_specs = (
        P("x", None),
        P(),
        P(None, None, head),
        P(None, head),
        P(head, None),
        P(),
        P(),
        P(every, None),
        P(None, None, every),
        P(every, None),
    )
    return jax.shard_map(body, mesh=fine, in_specs=in_specs, out_specs=P(every, None), check_vma=False)
```

```python
import math

import jax
import jax.numpy as jnp
from jax import lax
from jax.experimental import pallas as pl
from jax.experimental.pallas import tpu as pltpu
from jax.sharding import Mesh
from jax.sharding import PartitionSpec as P

HD = 128
D = 2048
STATE = 8256
EXPERTS = 64
TOP = 8
CAP = 3
SLAB = 16
HALF = 256
SHARD = 512
CHIP_AXES = ("x", "z", "y")


def swap_core(array):
    return lax.ppermute(array, "c", [(0, 1), (1, 0)])


def shift(array, axis, step):
    return lax.ppermute(array, axis, [(i, (i + step) % 4) for i in range(4)])


VMEM = pl.BlockSpec(memory_space=pltpu.VMEM)


def room(mebibytes):
    return pltpu.CompilerParams(vmem_limit_bytes=int(mebibytes * 1024 * 1024))


def cost(microseconds):
    return pl.CostEstimate(
        flops=int(microseconds * 1e9), bytes_accessed=int(microseconds * 3e6), transcendentals=0
    )


ROWS = EXPERTS * CAP
PIECES = D // 128
TILE_ROWS = ROWS * PIECES


def norm_scaled(values, gain):
    return values * lax.rsqrt(jnp.mean(values * values, axis=-1, keepdims=True) + 1e-06) * gain


GROUP = 8
TAIL_AT = 8064


def carried_kernel(m_ref, q_own_ref, q_other_ref, out_ref, q_ref, w_a, w_b, tail_ref):
    tail_ref[:, : STATE - TAIL_AT] = m_ref[:, TAIL_AT:]
    q_ref[:, :HALF] = q_own_ref[...].astype(jnp.float32)
    q_ref[:, HALF:] = q_other_ref[...].astype(jnp.float32)
    q_cols = jnp.concatenate([q_own_ref[...], q_other_ref[...]], axis=1)
    lane = lax.broadcasted_iota(jnp.int32, (64, 128), 1)
    root = math.sqrt(2.0)
    weights = (w_a, w_b)

    def prepare(number):
        base = number * GROUP
        for k in range(GROUP):
            i = base + k
            offset = 127 * i - (i * (i - 1)) // 2
            tile, turn = (offset // 128) * 128, offset % 128
            if tile < TAIL_AT:
                first, second = m_ref[:, tile : tile + 128], m_ref[:, tile + 128 : tile + 256]
            else:
                first, second = tail_ref[:, :128], tail_ref[:, 128:]
            if turn == 0:
                joined = first
            else:
                joined = jnp.where(
                    lane < 128 - turn,
                    pltpu.roll(first, 128 - turn, 1),
                    pltpu.roll(second, 128 - turn, 1),
                )
            weights[number % 2][64 * k : 64 * k + 64, :] = jnp.where(
                lane > i, joined * root, jnp.where(lane == i, joined, 0.0)
            ).astype(jnp.bfloat16)

    prepare(0)
    for number in range(HD // GROUP):
        spread = jnp.dot(weights[number % 2][...], q_cols, preferred_element_type=jnp.float32)
        if number + 1 < HD // GROUP:
            prepare(number + 1)
        base = number * GROUP
        total = spread[0:64] * q_ref[base : base + 1, :]
        for k in range(1, GROUP):
            total = total + spread[64 * k : 64 * k + 64] * q_ref[base + k : base + k + 1, :]
        if number == 0:
            out_ref[...] = total
        else:
            out_ref[...] += total


def carried_part(state_cols, q_own, q_other):
    return pl.pallas_call(
        carried_kernel,
        out_shape=jax.ShapeDtypeStruct((64, SHARD), jnp.float32),
        in_specs=[VMEM] * 3,
        out_specs=VMEM,
        scratch_shapes=[
            pltpu.VMEM((HD, SHARD), jnp.float32),
            pltpu.VMEM((64 * GROUP, HD), jnp.bfloat16),
            pltpu.VMEM((64 * GROUP, HD), jnp.bfloat16),
            pltpu.VMEM((64, 256), jnp.float32),
        ],
        compiler_params=room(2),
        cost_estimate=cost(5),
        name="carried",
    )(state_cols, q_own, q_other)


def window_kernel(q_own_ref, q_other_ref, kv0, kv1, kv2, kv3, carried_ref, mine_ref, send_ref):
    core, shard = lax.axis_index("c"), lax.axis_index("x")
    q_cols = jnp.concatenate([q_own_ref[...], q_other_ref[...]], axis=1)
    key = lax.broadcasted_iota(jnp.int32, (HALF, SHARD), 0)
    query = lax.broadcasted_iota(jnp.int32, (HALF, SHARD), 1)
    key_place = (key // 16) * 32 + key % 16 + core * 16
    inside = query % HALF
    query_place = (inside // 16) * 32 + inside % 16 + jnp.where(query < HALF, core, 1 - core) * 16
    allowed = key_place <= query_place
    total = jnp.zeros((HD, SHARD), jnp.float32)
    for number, kv in enumerate((kv0, kv1, kv2, kv3)):
        scores = lax.dot_general(
            kv[:HD, :], q_cols, (((0,), (0,)), ((), ())), preferred_element_type=jnp.float32
        )
        weights = scores * scores
        if number == 0:
            weights = jnp.where(allowed, weights, 0.0)
        else:
            weights = jnp.where(shard >= number, weights, 0.0)
        total = total + jnp.dot(
            kv[HD:, :], weights.astype(jnp.bfloat16), preferred_element_type=jnp.float32
        )
    upper = total[:64] + carried_ref[...]
    lower = total[64:]
    mine_ref[...] = jnp.concatenate([upper[:, :HALF], lower[:, :HALF]], axis=0).T
    send_ref[...] = jnp.concatenate([lower[:, HALF:], upper[:, HALF:]], axis=0).T.astype(jnp.bfloat16)


def window_part(q_own, q_other, kvs, carried):
    return pl.pallas_call(
        window_kernel,
        out_shape=(
            jax.ShapeDtypeStruct((HALF, HD), jnp.float32),
            jax.ShapeDtypeStruct((HALF, HD), jnp.bfloat16),
        ),
        in_specs=[VMEM] * 7,
        out_specs=(VMEM,) * 2,
        compiler_params=room(2),
        cost_estimate=cost(2),
        name="window",
    )(q_own, q_other, *kvs, carried)


def norm_kernel(tokens_ref, gain_ref, out_ref, slab_ref):
    core = lax.axis_index("c")
    slab_ref[...] = tokens_ref[lax.axis_index("z") * 4 + lax.axis_index("y"), core]
    for k in range(4):
        floats = tokens_ref[4 * k : 4 * k + 4, core].astype(jnp.float32).reshape(64, D)
        out_ref[64 * k : 64 * k + 64, :] = norm_scaled(floats, gain_ref[...]).astype(jnp.bfloat16)


def norm_part(tokens, gain):
    return pl.pallas_call(
        norm_kernel,
        out_shape=(
            jax.ShapeDtypeStruct((HALF, D), jnp.bfloat16),
            jax.ShapeDtypeStruct((SLAB, D), jnp.bfloat16),
        ),
        in_specs=[VMEM, VMEM],
        out_specs=(VMEM, VMEM),
        compiler_params=room(2),
        cost_estimate=cost(1),
        name="norm",
    )(tokens.reshape(16, 2, 16, D), gain.reshape(1, D))


def project_kernel(normed_ref, own_ref, other_ref, q_ref, kv_ref):
    core = lax.axis_index("c")
    normed = normed_ref[...]

    def times(ref):
        return lax.dot_general(
            ref[...].reshape(192, D),
            normed,
            (((1,), (1,)), ((), ())),
            preferred_element_type=jnp.float32,
        ).astype(jnp.bfloat16)

    own, other = times(own_ref), times(other_ref)
    own_at = pl.multiple_of(core * 64, 64)
    other_at = pl.multiple_of((1 - core) * 64, 64)
    q_ref[pl.ds(own_at, 64), :] = own[:64]
    q_ref[pl.ds(other_at, 64), :] = other[:64]
    kv_ref[pl.ds(own_at, 64), :] = own[64:128]
    kv_ref[pl.ds(other_at, 64), :] = other[64:128]
    kv_ref[128:192, :] = own[128:]
    kv_ref[192:256, :] = other[128:]


def project_part(normed, own, other):
    return pl.pallas_call(
        project_kernel,
        out_shape=(
            jax.ShapeDtypeStruct((HD, HALF), jnp.bfloat16),
            jax.ShapeDtypeStruct((2 * HD, HALF), jnp.bfloat16),
        ),
        in_specs=[VMEM, VMEM, VMEM],
        out_specs=(VMEM, VMEM),
        compiler_params=room(2),
        cost_estimate=cost(1),
        name="project",
    )(normed, own, other)


def attend_kernel(mine_ref, received_ref, *rest):
    outs, scratch = rest[:4], rest[4]
    raw = (mine_ref[...] + received_ref[...].astype(jnp.float32)) / HD
    scratch[...] = norm_scaled(raw, 1.0).reshape(4, 64, HD)
    for step, out in enumerate(outs):
        at = pl.multiple_of(lax.rem(lax.axis_index("y") + step, 4) * SLAB, SLAB)
        out[...] = scratch[:, pl.ds(at, SLAB), :].reshape(64, HD).astype(jnp.bfloat16)


def attend_part(mine, received):
    return pl.pallas_call(
        attend_kernel,
        out_shape=(jax.ShapeDtypeStruct((64, HD), jnp.bfloat16),) * 4,
        in_specs=[VMEM, VMEM],
        out_specs=(VMEM,) * 4,
        scratch_shapes=[pltpu.VMEM((4, 64, HD), jnp.float32)],
        compiler_params=room(2),
        cost_estimate=cost(0.7),
        name="attend",
    )(mine, received)


def pack_kernel(*refs):
    for step in range(4):
        refs[4][64 * step : 64 * step + 64, :] = refs[step][...]


def pack_part(rows):
    return pl.pallas_call(
        pack_kernel,
        out_shape=jax.ShapeDtypeStruct((HALF, D), jnp.bfloat16),
        in_specs=[VMEM] * 4,
        out_specs=VMEM,
        compiler_params=room(2),
        cost_estimate=cost(0.5),
        name="pack",
    )(*rows)


def output_kernel(*rest):
    pieces, own, other, outs, scratch = rest[:4], rest[4], rest[5], rest[6:10], rest[10]
    loaded = [piece[...] for piece in pieces]
    for at in range(0, D, 512):
        total = jnp.zeros((64, 512), jnp.float32)
        for step in range(4):
            total = total + jnp.dot(
                loaded[step][:, :64],
                own[64 * step : 64 * step + 64, at : at + 512],
                preferred_element_type=jnp.float32,
            )
            total = total + jnp.dot(
                loaded[step][:, 64:],
                other[64 * step : 64 * step + 64, at : at + 512],
                preferred_element_type=jnp.float32,
            )
        scratch[:, at : at + 512] = total
    for step, out in enumerate(outs):
        at = pl.multiple_of(lax.rem(lax.axis_index("z") + step, 4) * SLAB, SLAB)
        out[...] = scratch[pl.ds(at, SLAB), :].astype(out.dtype)


def output_part(pieces, own, other):
    return pl.pallas_call(
        output_kernel,
        out_shape=(jax.ShapeDtypeStruct((SLAB, D), jnp.float32),)
        + (jax.ShapeDtypeStruct((SLAB, D), jnp.bfloat16),) * 3,
        in_specs=[VMEM] * 6,
        out_specs=(VMEM,) * 4,
        scratch_shapes=[pltpu.VMEM((64, D), jnp.float32)],
        compiler_params=room(2),
        cost_estimate=cost(2),
        name="output",
    )(*pieces, own, other)


def map_kernel(index_ref, gain_ref, rows_ref, lanes_ref, gain_out):
    gain_out[...] = gain_ref[...]
    index = index_ref[...]
    expert = lax.broadcasted_iota(jnp.int32, (EXPERTS, SLAB), 0)
    chosen = jnp.zeros((EXPERTS, SLAB), jnp.float32)
    for k in range(TOP):
        chosen = chosen + jnp.where(index[k : k + 1, :] == expert, 1.0, 0.0)
    before = lax.broadcasted_iota(jnp.int32, (SLAB, SLAB), 0) < lax.broadcasted_iota(
        jnp.int32, (SLAB, SLAB), 1
    )
    slot = jnp.dot(
        chosen.astype(jnp.bfloat16),
        jnp.where(before, 1.0, 0.0).astype(jnp.bfloat16),
        preferred_element_type=jnp.float32,
    )
    code = jnp.where(chosen > 0.5, slot, -1.0).astype(jnp.bfloat16)
    lane = lax.broadcasted_iota(jnp.int32, (SLAB, TILE_ROWS), 1)
    wide = lax.dot_general(
        code, spread_map(), (((0,), (0,)), ((), ())), preferred_element_type=jnp.float32
    )
    lanes_ref[...] = jnp.where(
        wide == ((lane // PIECES) % CAP).astype(jnp.float32), 1.0, 0.0
    )
    token = lax.broadcasted_iota(jnp.int32, (SLAB, 256), 0)
    column = lax.broadcasted_iota(jnp.int32, (SLAB, 256), 1)
    by_column = jnp.dot(
        code,
        jnp.where(column % SLAB == token, 1.0, 0.0).astype(jnp.bfloat16),
        preferred_element_type=jnp.float32,
    ).astype(jnp.bfloat16)
    row_expert = lax.broadcasted_iota(jnp.int32, (TILE_ROWS, EXPERTS), 0) // (CAP * PIECES)
    pick = jnp.where(
        row_expert == lax.broadcasted_iota(jnp.int32, (TILE_ROWS, EXPERTS), 1), 1.0, 0.0
    ).astype(jnp.bfloat16)
    tall = jnp.dot(pick, by_column, preferred_element_type=jnp.float32)
    row = lax.broadcasted_iota(jnp.int32, (TILE_ROWS, 256), 0)
    piece = lax.broadcasted_iota(jnp.int32, (TILE_ROWS, 256), 1) // SLAB
    rows_ref[...] = jnp.where(
        (tall == ((row // PIECES) % CAP).astype(jnp.float32)) & (row % PIECES == piece), 1.0, 0.0
    ).astype(jnp.bfloat16)


def spread_map():
    lane_expert = lax.broadcasted_iota(jnp.int32, (EXPERTS, TILE_ROWS), 1) // (CAP * PIECES)
    return jnp.where(
        lane_expert == lax.broadcasted_iota(jnp.int32, (EXPERTS, TILE_ROWS), 0), 1.0, 0.0
    ).astype(jnp.bfloat16)


def map_part(index, gain):
    return pl.pallas_call(
        map_kernel,
        out_shape=(
            jax.ShapeDtypeStruct((TILE_ROWS, 256), jnp.bfloat16),
            jax.ShapeDtypeStruct((SLAB, TILE_ROWS), jnp.float32),
            jax.ShapeDtypeStruct((1, D), jnp.float32),
        ),
        in_specs=[VMEM, VMEM],
        out_specs=(VMEM,) * 3,
        compiler_params=room(14),
        cost_estimate=cost(2),
        name="maps",
    )(index, gain.reshape(1, D))


def dispatch_kernel(
    slab_ref, own_ref, r1, r2, r3, gain_ref, router_ref, rows_ref, lanes_ref, residual_ref, out_ref, wide_ref
):
    residual = slab_ref[...].astype(jnp.float32) + own_ref[...]
    for received in (r1, r2, r3):
        residual = residual + received[...].astype(jnp.float32)
    residual_ref[...] = residual
    inputs = norm_scaled(residual, gain_ref[...]).astype(jnp.bfloat16)
    logits = lax.dot_general(
        inputs, router_ref[...], (((1,), (1,)), ((), ())), preferred_element_type=jnp.float32
    )
    wide_ref[...] = lanes_ref[...] * jnp.dot(
        jax.nn.sigmoid(logits).astype(jnp.bfloat16),
        spread_map(),
        preferred_element_type=jnp.float32,
    )
    tall = jnp.concatenate([inputs[:, at : at + 128] for at in range(0, D, 128)], axis=0)
    out_ref[...] = jnp.dot(rows_ref[...], tall, preferred_element_type=jnp.float32).astype(
        jnp.bfloat16
    )


def dispatch_part(slab, own, received, gain, router, rows, lanes):
    return pl.pallas_call(
        dispatch_kernel,
        out_shape=(
            jax.ShapeDtypeStruct((SLAB, D), jnp.float32),
            jax.ShapeDtypeStruct((TILE_ROWS, 128), jnp.bfloat16),
            jax.ShapeDtypeStruct((SLAB, TILE_ROWS), jnp.float32),
        ),
        in_specs=[VMEM] * 9,
        out_specs=(VMEM,) * 3,
        compiler_params=room(6),
        cost_estimate=cost(1),
        name="dispatch",
    )(slab, own, *received, gain, router, rows, lanes)


def expert_kernel(
    rows_ref, first_own, second_own, first_other, second_other, out_ref, flat_ref, input_ref, total_ref
):
    flat_ref[...] = rows_ref[...].astype(jnp.float32)
    for at in range(PIECES):
        input_ref[:, at * 128 : (at + 1) * 128] = flat_ref[
            pl.ds(at, ROWS, stride=PIECES), :
        ].astype(jnp.bfloat16)
    for piece, (first, second) in enumerate(
        ((first_own, second_own), (first_other, second_other))
    ):
        gate = jnp.dot(input_ref[...], first[0], preferred_element_type=jnp.float32)
        up = jnp.dot(input_ref[...], first[1], preferred_element_type=jnp.float32)
        hidden = (gate / (1.0 + jnp.exp(-gate)) * up).astype(jnp.bfloat16)
        product = jnp.dot(hidden, second[...], preferred_element_type=jnp.float32)
        if piece == 0:
            total_ref[...] = product
        else:
            product = product + total_ref[...]
            for at in range(PIECES):
                flat_ref[pl.ds(at, ROWS, stride=PIECES), :] = product[:, at * 128 : (at + 1) * 128]
    out_ref[...] = flat_ref[...].astype(jnp.bfloat16)


def expert_part(rows, first, second, first_other, second_other):
    return pl.pallas_call(
        expert_kernel,
        out_shape=jax.ShapeDtypeStruct((TILE_ROWS, 128), jnp.bfloat16),
        in_specs=[VMEM] * 5,
        out_specs=VMEM,
        scratch_shapes=[
            pltpu.VMEM((TILE_ROWS, 128), jnp.float32),
            pltpu.VMEM((ROWS, D), jnp.bfloat16),
            pltpu.VMEM((ROWS, D), jnp.float32),
        ],
        compiler_params=room(28),
        cost_estimate=cost(5),
        name="experts",
    )(rows, first, second, first_other, second_other)


def combine_kernel(residual_ref, wide_ref, rows_ref, out_ref, map_ref):
    wide = wide_ref[...]
    piece = lax.broadcasted_iota(jnp.int32, (SLAB, TILE_ROWS), 1) % PIECES
    for at in range(PIECES):
        map_ref[at * SLAB : (at + 1) * SLAB, :] = jnp.where(piece == at, wide, 0.0).astype(
            jnp.bfloat16
        )
    tall = jnp.dot(map_ref[...], rows_ref[...], preferred_element_type=jnp.float32)
    for at in range(PIECES):
        columns = slice(at * 128, (at + 1) * 128)
        out_ref[:, columns] = (
            residual_ref[:, columns] + tall[at * SLAB : (at + 1) * SLAB, :]
        ).astype(jnp.bfloat16)


def combine_part(residual, wide, rows):
    return pl.pallas_call(
        combine_kernel,
        out_shape=jax.ShapeDtypeStruct((SLAB, D), jnp.bfloat16),
        in_specs=[VMEM] * 3,
        out_specs=VMEM,
        scratch_shapes=[pltpu.VMEM((256, TILE_ROWS), jnp.bfloat16)],
        compiler_params=room(6),
        cost_estimate=cost(1),
        name="combine",
    )(residual, wide, rows)


def chips(rows):
    shaped = rows.reshape(EXPERTS, CAP * PIECES, 128)
    return lax.all_to_all(shaped, CHIP_AXES, split_axis=0, concat_axis=0, tiled=True).reshape(
        TILE_ROWS, 128
    )


def body(
    tokens,
    attention_gain,
    head_weights,
    carried_state,
    output_weight,
    expert_gain,
    router_weight,
    expert_index,
    expert_first,
    expert_second,
):
    own_weights = head_weights.transpose(0, 2, 1)
    other_weights = swap_core(own_weights)
    output_own = [output_weight] + [shift(output_weight, "y", step) for step in (1, 2, 3)]
    normed, slab = norm_part(tokens, attention_gain)
    q_own, kv = project_part(normed, own_weights, other_weights)
    kvs = [kv] + [shift(kv, "x", step) for step in (1, 2, 3)]
    q_other = swap_core(q_own)
    rows_map, lanes_map, gain = map_part(expert_index.T, expert_gain)

    carried = carried_part(carried_state.T, q_own, q_other)
    mine, send = window_part(q_own, q_other, kvs, carried)
    tied = lax.optimization_barrier((swap_core(send), expert_first, expert_second, *output_own))
    received, output_own = tied[0], pack_part(tied[3:])
    first_other, second_other = swap_core(tied[1]), swap_core(tied[2])
    output_other = swap_core(output_own)
    pieces = attend_part(mine, received)
    pieces = [pieces[0]] + [shift(pieces[step], "y", step) for step in (1, 2, 3)]
    sums = output_part(pieces, output_own, output_other)
    summed = [shift(sums[step], "z", step) for step in (1, 2, 3)]
    residual, outgoing, wide = dispatch_part(
        slab, sums[0], summed, gain, router_weight.T, rows_map, lanes_map
    )
    arrived = chips(outgoing)
    produced = expert_part(arrived, expert_first, expert_second, first_other, second_other)
    return combine_part(residual, wide, chips(produced))


def solution(mesh):
    fine = Mesh(mesh.devices.reshape(4, 4, 4, 2), ("x", "z", "y", "c"))
    head = ("z", "y", "c")
    every = ("x", "z", "y", "c")
    in_specs = (
        P("x", None),
        P(),
        P(None, None, head),
        P(None, head),
        P(head, None),
        P(),
        P(),
        P(every, None),
        P(None, None, every),
        P(every, None),
    )
    return jax.shard_map(body, mesh=fine, in_specs=in_specs, out_specs=P(every, None), check_vma=False)
```

```python
import math

import jax
import jax.numpy as jnp
from jax import lax
from jax.experimental import pallas as pl
from jax.experimental.pallas import tpu as pltpu
from jax.sharding import Mesh
from jax.sharding import PartitionSpec as P

HD = 128
D = 2048
STATE = 8256
EXPERTS = 64
TOP = 8
CAP = 3
SLAB = 16
HALF = 256
SHARD = 512
CHIP_AXES = ("x", "z", "y")


def swap_core(array):
    return lax.ppermute(array, "c", [(0, 1), (1, 0)])


def shift(array, axis, step):
    return lax.ppermute(array, axis, [(i, (i + step) % 4) for i in range(4)])


VMEM = pl.BlockSpec(memory_space=pltpu.VMEM)


def room(mebibytes):
    return pltpu.CompilerParams(vmem_limit_bytes=int(mebibytes * 1024 * 1024))


def cost(microseconds):
    return pl.CostEstimate(
        flops=int(microseconds * 1e9), bytes_accessed=int(microseconds * 3e6), transcendentals=0
    )


ROWS = EXPERTS * CAP
PIECES = D // 128
TILE_ROWS = ROWS * PIECES


def norm_scaled(values, gain):
    return values * lax.rsqrt(jnp.mean(values * values, axis=-1, keepdims=True) + 1e-06) * gain


GROUP = 8
TAIL_AT = 8064


def carried_kernel(m_ref, q_own_ref, q_other_ref, out_ref, q_ref, w_a, w_b, tail_ref):
    tail_ref[:, : STATE - TAIL_AT] = m_ref[:, TAIL_AT:]
    q_ref[:, :HALF] = q_own_ref[...].astype(jnp.float32)
    q_ref[:, HALF:] = q_other_ref[...].astype(jnp.float32)
    q_cols = jnp.concatenate([q_own_ref[...], q_other_ref[...]], axis=1)
    lane = lax.broadcasted_iota(jnp.int32, (64, 128), 1)
    root = math.sqrt(2.0)
    weights = (w_a, w_b)

    def prepare(number):
        base = number * GROUP
        for k in range(GROUP):
            i = base + k
            offset = 127 * i - (i * (i - 1)) // 2
            tile, turn = (offset // 128) * 128, offset % 128
            if tile < TAIL_AT:
                first, second = m_ref[:, tile : tile + 128], m_ref[:, tile + 128 : tile + 256]
            else:
                first, second = tail_ref[:, :128], tail_ref[:, 128:]
            if turn == 0:
                joined = first
            else:
                joined = jnp.where(
                    lane < 128 - turn,
                    pltpu.roll(first, 128 - turn, 1),
                    pltpu.roll(second, 128 - turn, 1),
                )
            weights[number % 2][64 * k : 64 * k + 64, :] = jnp.where(
                lane > i, joined * root, jnp.where(lane == i, joined, 0.0)
            ).astype(jnp.bfloat16)

    prepare(0)
    for number in range(HD // GROUP):
        spread = jnp.dot(weights[number % 2][...], q_cols, preferred_element_type=jnp.float32)
        if number + 1 < HD // GROUP:
            prepare(number + 1)
        base = number * GROUP
        total = spread[0:64] * q_ref[base : base + 1, :]
        for k in range(1, GROUP):
            total = total + spread[64 * k : 64 * k + 64] * q_ref[base + k : base + k + 1, :]
        if number == 0:
            out_ref[...] = total
        else:
            out_ref[...] += total


def carried_part(state_cols, q_own, q_other):
    return pl.pallas_call(
        carried_kernel,
        out_shape=jax.ShapeDtypeStruct((64, SHARD), jnp.float32),
        in_specs=[VMEM] * 3,
        out_specs=VMEM,
        scratch_shapes=[
            pltpu.VMEM((HD, SHARD), jnp.float32),
            pltpu.VMEM((64 * GROUP, HD), jnp.bfloat16),
            pltpu.VMEM((64 * GROUP, HD), jnp.bfloat16),
            pltpu.VMEM((64, 256), jnp.float32),
        ],
        compiler_params=room(2),
        cost_estimate=cost(5),
        name="carried",
    )(state_cols, q_own, q_other)


def window_kernel(q_own_ref, q_other_ref, kv0, kv1, kv2, kv3, carried_ref, mine_ref, send_ref):
    core, shard = lax.axis_index("c"), lax.axis_index("x")
    q_cols = jnp.concatenate([q_own_ref[...], q_other_ref[...]], axis=1)
    key = lax.broadcasted_iota(jnp.int32, (HALF, SHARD), 0)
    query = lax.broadcasted_iota(jnp.int32, (HALF, SHARD), 1)
    key_place = (key // 16) * 32 + key % 16 + core * 16
    inside = query % HALF
    query_place = (inside // 16) * 32 + inside % 16 + jnp.where(query < HALF, core, 1 - core) * 16
    allowed = key_place <= query_place
    total = jnp.zeros((HD, SHARD), jnp.float32)
    for number, kv in enumerate((kv0, kv1, kv2, kv3)):
        scores = lax.dot_general(
            kv[:HD, :], q_cols, (((0,), (0,)), ((), ())), preferred_element_type=jnp.float32
        )
        weights = scores * scores
        if number == 0:
            weights = jnp.where(allowed, weights, 0.0)
        else:
            weights = jnp.where(shard >= number, weights, 0.0)
        total = total + jnp.dot(
            kv[HD:, :], weights.astype(jnp.bfloat16), preferred_element_type=jnp.float32
        )
    upper = total[:64] + carried_ref[...]
    lower = total[64:]
    mine_ref[...] = jnp.concatenate([upper[:, :HALF], lower[:, :HALF]], axis=0).T
    send_ref[...] = jnp.concatenate([lower[:, HALF:], upper[:, HALF:]], axis=0).T.astype(jnp.bfloat16)


def window_part(q_own, q_other, kvs, carried):
    return pl.pallas_call(
        window_kernel,
        out_shape=(
            jax.ShapeDtypeStruct((HALF, HD), jnp.float32),
            jax.ShapeDtypeStruct((HALF, HD), jnp.bfloat16),
        ),
        in_specs=[VMEM] * 7,
        out_specs=(VMEM,) * 2,
        compiler_params=room(2),
        cost_estimate=cost(2),
        name="window",
    )(q_own, q_other, *kvs, carried)


def norm_kernel(tokens_ref, out_ref, slab_ref):
    core = lax.axis_index("c")
    slab_ref[...] = tokens_ref[lax.axis_index("z") * 4 + lax.axis_index("y"), core]
    for k in range(4):
        floats = tokens_ref[4 * k : 4 * k + 4, core].astype(jnp.float32).reshape(64, D)
        out_ref[64 * k : 64 * k + 64, :] = norm_scaled(floats, 1.0)


def norm_part(tokens):
    return pl.pallas_call(
        norm_kernel,
        out_shape=(
            jax.ShapeDtypeStruct((HALF, D), jnp.float32),
            jax.ShapeDtypeStruct((SLAB, D), jnp.bfloat16),
        ),
        in_specs=[VMEM],
        out_specs=(VMEM, VMEM),
        compiler_params=room(2),
        cost_estimate=cost(1),
        name="norm",
    )(tokens.reshape(16, 2, 16, D))


def project_kernel(normed_ref, gain_ref, own_ref, other_ref, q_ref, kv_ref):
    core = lax.axis_index("c")
    normed = (normed_ref[...] * gain_ref[...]).astype(jnp.bfloat16)

    def times(ref):
        return lax.dot_general(
            ref[...].reshape(192, D),
            normed,
            (((1,), (1,)), ((), ())),
            preferred_element_type=jnp.float32,
        ).astype(jnp.bfloat16)

    own, other = times(own_ref), times(other_ref)
    own_at = pl.multiple_of(core * 64, 64)
    other_at = pl.multiple_of((1 - core) * 64, 64)
    q_ref[pl.ds(own_at, 64), :] = own[:64]
    q_ref[pl.ds(other_at, 64), :] = other[:64]
    kv_ref[pl.ds(own_at, 64), :] = own[64:128]
    kv_ref[pl.ds(other_at, 64), :] = other[64:128]
    kv_ref[128:192, :] = own[128:]
    kv_ref[192:256, :] = other[128:]


def project_part(normed, gain, own, other):
    return pl.pallas_call(
        project_kernel,
        out_shape=(
            jax.ShapeDtypeStruct((HD, HALF), jnp.bfloat16),
            jax.ShapeDtypeStruct((2 * HD, HALF), jnp.bfloat16),
        ),
        in_specs=[VMEM] * 4,
        out_specs=(VMEM, VMEM),
        compiler_params=room(4),
        cost_estimate=cost(1),
        name="project",
    )(normed, gain.reshape(1, D), own, other)


def attend_kernel(mine_ref, received_ref, *rest):
    outs, scratch = rest[:4], rest[4]
    raw = (mine_ref[...] + received_ref[...].astype(jnp.float32)) / HD
    scratch[...] = norm_scaled(raw, 1.0).reshape(4, 64, HD)
    for step, out in enumerate(outs):
        at = pl.multiple_of(lax.rem(lax.axis_index("y") + step, 4) * SLAB, SLAB)
        out[...] = scratch[:, pl.ds(at, SLAB), :].reshape(64, HD).astype(jnp.bfloat16)


def attend_part(mine, received):
    return pl.pallas_call(
        attend_kernel,
        out_shape=(jax.ShapeDtypeStruct((64, HD), jnp.bfloat16),) * 4,
        in_specs=[VMEM, VMEM],
        out_specs=(VMEM,) * 4,
        scratch_shapes=[pltpu.VMEM((4, 64, HD), jnp.float32)],
        compiler_params=room(2),
        cost_estimate=cost(0.7),
        name="attend",
    )(mine, received)


def pack_kernel(*refs):
    for step in range(4):
        refs[4][64 * step : 64 * step + 64, :] = refs[step][...]


def pack_part(rows):
    return pl.pallas_call(
        pack_kernel,
        out_shape=jax.ShapeDtypeStruct((HALF, D), jnp.bfloat16),
        in_specs=[VMEM] * 4,
        out_specs=VMEM,
        compiler_params=room(2),
        cost_estimate=cost(0.5),
        name="pack",
    )(*rows)


def output_kernel(*rest):
    pieces, own, other, outs, scratch = rest[:4], rest[4], rest[5], rest[6:10], rest[10]
    loaded = [piece[...] for piece in pieces]
    for at in range(0, D, 512):
        total = jnp.zeros((64, 512), jnp.float32)
        for step in range(4):
            total = total + jnp.dot(
                loaded[step][:, :64],
                own[64 * step : 64 * step + 64, at : at + 512],
                preferred_element_type=jnp.float32,
            )
            total = total + jnp.dot(
                loaded[step][:, 64:],
                other[64 * step : 64 * step + 64, at : at + 512],
                preferred_element_type=jnp.float32,
            )
        scratch[:, at : at + 512] = total
    for step, out in enumerate(outs):
        at = pl.multiple_of(lax.rem(lax.axis_index("z") + step, 4) * SLAB, SLAB)
        out[...] = scratch[pl.ds(at, SLAB), :].astype(out.dtype)


def output_part(pieces, own, other):
    return pl.pallas_call(
        output_kernel,
        out_shape=(jax.ShapeDtypeStruct((SLAB, D), jnp.float32),)
        + (jax.ShapeDtypeStruct((SLAB, D), jnp.bfloat16),) * 3,
        in_specs=[VMEM] * 6,
        out_specs=(VMEM,) * 4,
        scratch_shapes=[pltpu.VMEM((64, D), jnp.float32)],
        compiler_params=room(2),
        cost_estimate=cost(2),
        name="output",
    )(*pieces, own, other)


def map_kernel(index_ref, gain_ref, rows_ref, lanes_ref, gain_out):
    gain_out[...] = gain_ref[...]
    index = index_ref[...]
    expert = lax.broadcasted_iota(jnp.int32, (EXPERTS, SLAB), 0)
    chosen = jnp.zeros((EXPERTS, SLAB), jnp.float32)
    for k in range(TOP):
        chosen = chosen + jnp.where(index[k : k + 1, :] == expert, 1.0, 0.0)
    before = lax.broadcasted_iota(jnp.int32, (SLAB, SLAB), 0) < lax.broadcasted_iota(
        jnp.int32, (SLAB, SLAB), 1
    )
    slot = jnp.dot(
        chosen.astype(jnp.bfloat16),
        jnp.where(before, 1.0, 0.0).astype(jnp.bfloat16),
        preferred_element_type=jnp.float32,
    )
    code = jnp.where(chosen > 0.5, slot, -1.0).astype(jnp.bfloat16)
    lane = lax.broadcasted_iota(jnp.int32, (SLAB, TILE_ROWS), 1)
    wide = lax.dot_general(
        code, spread_map(), (((0,), (0,)), ((), ())), preferred_element_type=jnp.float32
    )
    lanes_ref[...] = jnp.where(
        wide == ((lane // PIECES) % CAP).astype(jnp.float32), 1.0, 0.0
    )
    token = lax.broadcasted_iota(jnp.int32, (SLAB, 256), 0)
    column = lax.broadcasted_iota(jnp.int32, (SLAB, 256), 1)
    by_column = jnp.dot(
        code,
        jnp.where(column % SLAB == token, 1.0, 0.0).astype(jnp.bfloat16),
        preferred_element_type=jnp.float32,
    ).astype(jnp.bfloat16)
    row_expert = lax.broadcasted_iota(jnp.int32, (TILE_ROWS, EXPERTS), 0) // (CAP * PIECES)
    pick = jnp.where(
        row_expert == lax.broadcasted_iota(jnp.int32, (TILE_ROWS, EXPERTS), 1), 1.0, 0.0
    ).astype(jnp.bfloat16)
    tall = jnp.dot(pick, by_column, preferred_element_type=jnp.float32)
    row = lax.broadcasted_iota(jnp.int32, (TILE_ROWS, 256), 0)
    piece = lax.broadcasted_iota(jnp.int32, (TILE_ROWS, 256), 1) // SLAB
    rows_ref[...] = jnp.where(
        (tall == ((row // PIECES) % CAP).astype(jnp.float32)) & (row % PIECES == piece), 1.0, 0.0
    ).astype(jnp.bfloat16)


def spread_map():
    lane_expert = lax.broadcasted_iota(jnp.int32, (EXPERTS, TILE_ROWS), 1) // (CAP * PIECES)
    return jnp.where(
        lane_expert == lax.broadcasted_iota(jnp.int32, (EXPERTS, TILE_ROWS), 0), 1.0, 0.0
    ).astype(jnp.bfloat16)


def map_part(index, gain):
    return pl.pallas_call(
        map_kernel,
        out_shape=(
            jax.ShapeDtypeStruct((TILE_ROWS, 256), jnp.bfloat16),
            jax.ShapeDtypeStruct((SLAB, TILE_ROWS), jnp.float32),
            jax.ShapeDtypeStruct((1, D), jnp.float32),
        ),
        in_specs=[VMEM, VMEM],
        out_specs=(VMEM,) * 3,
        compiler_params=room(14),
        cost_estimate=cost(2),
        name="maps",
    )(index, gain.reshape(1, D))


def dispatch_kernel(
    slab_ref, own_ref, r1, r2, r3, gain_ref, router_ref, rows_ref, lanes_ref, residual_ref, out_ref, wide_ref
):
    residual = slab_ref[...].astype(jnp.float32) + own_ref[...]
    for received in (r1, r2, r3):
        residual = residual + received[...].astype(jnp.float32)
    residual_ref[...] = residual
    inputs = norm_scaled(residual, gain_ref[...]).astype(jnp.bfloat16)
    logits = lax.dot_general(
        inputs, router_ref[...], (((1,), (1,)), ((), ())), preferred_element_type=jnp.float32
    )
    wide_ref[...] = lanes_ref[...] * jnp.dot(
        jax.nn.sigmoid(logits).astype(jnp.bfloat16),
        spread_map(),
        preferred_element_type=jnp.float32,
    )
    tall = jnp.concatenate([inputs[:, at : at + 128] for at in range(0, D, 128)], axis=0)
    out_ref[...] = jnp.dot(rows_ref[...], tall, preferred_element_type=jnp.float32).astype(
        jnp.bfloat16
    )


def dispatch_part(slab, own, received, gain, router, rows, lanes):
    return pl.pallas_call(
        dispatch_kernel,
        out_shape=(
            jax.ShapeDtypeStruct((SLAB, D), jnp.float32),
            jax.ShapeDtypeStruct((TILE_ROWS, 128), jnp.bfloat16),
            jax.ShapeDtypeStruct((SLAB, TILE_ROWS), jnp.float32),
        ),
        in_specs=[VMEM] * 9,
        out_specs=(VMEM,) * 3,
        compiler_params=room(6),
        cost_estimate=cost(1),
        name="dispatch",
    )(slab, own, *received, gain, router, rows, lanes)


def expert_kernel(
    rows_ref, first_own, second_own, first_other, second_other, out_ref, flat_ref, input_ref, total_ref
):
    flat_ref[...] = rows_ref[...].astype(jnp.float32)
    for at in range(PIECES):
        input_ref[:, at * 128 : (at + 1) * 128] = flat_ref[
            pl.ds(at, ROWS, stride=PIECES), :
        ].astype(jnp.bfloat16)
    for piece, (first, second) in enumerate(
        ((first_own, second_own), (first_other, second_other))
    ):
        gate = jnp.dot(input_ref[...], first[0], preferred_element_type=jnp.float32)
        up = jnp.dot(input_ref[...], first[1], preferred_element_type=jnp.float32)
        hidden = (gate / (1.0 + jnp.exp(-gate)) * up).astype(jnp.bfloat16)
        product = jnp.dot(hidden, second[...], preferred_element_type=jnp.float32)
        if piece == 0:
            total_ref[...] = product
        else:
            product = product + total_ref[...]
            for at in range(PIECES):
                flat_ref[pl.ds(at, ROWS, stride=PIECES), :] = product[:, at * 128 : (at + 1) * 128]
    out_ref[...] = flat_ref[...].astype(jnp.bfloat16)


def expert_part(rows, first, second, first_other, second_other):
    return pl.pallas_call(
        expert_kernel,
        out_shape=jax.ShapeDtypeStruct((TILE_ROWS, 128), jnp.bfloat16),
        in_specs=[VMEM] * 5,
        out_specs=VMEM,
        scratch_shapes=[
            pltpu.VMEM((TILE_ROWS, 128), jnp.float32),
            pltpu.VMEM((ROWS, D), jnp.bfloat16),
            pltpu.VMEM((ROWS, D), jnp.float32),
        ],
        compiler_params=room(28),
        cost_estimate=cost(5),
        name="experts",
    )(rows, first, second, first_other, second_other)


def combine_kernel(residual_ref, wide_ref, rows_ref, out_ref, map_ref):
    wide = wide_ref[...]
    piece = lax.broadcasted_iota(jnp.int32, (SLAB, TILE_ROWS), 1) % PIECES
    for at in range(PIECES):
        map_ref[at * SLAB : (at + 1) * SLAB, :] = jnp.where(piece == at, wide, 0.0).astype(
            jnp.bfloat16
        )
    tall = jnp.dot(map_ref[...], rows_ref[...], preferred_element_type=jnp.float32)
    for at in range(PIECES):
        columns = slice(at * 128, (at + 1) * 128)
        out_ref[:, columns] = (
            residual_ref[:, columns] + tall[at * SLAB : (at + 1) * SLAB, :]
        ).astype(jnp.bfloat16)


def combine_part(residual, wide, rows):
    return pl.pallas_call(
        combine_kernel,
        out_shape=jax.ShapeDtypeStruct((SLAB, D), jnp.bfloat16),
        in_specs=[VMEM] * 3,
        out_specs=VMEM,
        scratch_shapes=[pltpu.VMEM((256, TILE_ROWS), jnp.bfloat16)],
        compiler_params=room(6),
        cost_estimate=cost(1),
        name="combine",
    )(residual, wide, rows)


def chips(rows):
    shaped = rows.reshape(EXPERTS, CAP * PIECES, 128)
    return lax.all_to_all(shaped, CHIP_AXES, split_axis=0, concat_axis=0, tiled=True).reshape(
        TILE_ROWS, 128
    )


def body(
    tokens,
    attention_gain,
    head_weights,
    carried_state,
    output_weight,
    expert_gain,
    router_weight,
    expert_index,
    expert_first,
    expert_second,
):
    own_weights = head_weights.transpose(0, 2, 1)
    other_weights = swap_core(own_weights)
    normed, slab = norm_part(tokens)
    q_own, kv = project_part(normed, attention_gain, own_weights, other_weights)
    kvs = [kv] + [shift(kv, "x", step) for step in (1, 2, 3)]
    gathered = {step: shift(output_weight, "y", step) for step in (1, 3, 2)}
    output_own = [output_weight, gathered[1], gathered[2], gathered[3]]
    q_other = swap_core(q_own)
    rows_map, lanes_map, gain = map_part(expert_index.T, expert_gain)

    carried = carried_part(carried_state.T, q_own, q_other)
    mine, send = window_part(q_own, q_other, kvs, carried)
    tied = lax.optimization_barrier((swap_core(send), expert_first, expert_second, *output_own))
    received, output_own = tied[0], pack_part(tied[3:])
    first_other, second_other = swap_core(tied[1]), swap_core(tied[2])
    output_other = swap_core(output_own)
    pieces = attend_part(mine, received)
    pieces = [pieces[0]] + [shift(pieces[step], "y", step) for step in (1, 2, 3)]
    sums = output_part(pieces, output_own, output_other)
    summed = [shift(sums[step], "z", step) for step in (1, 2, 3)]
    residual, outgoing, wide = dispatch_part(
        slab, sums[0], summed, gain, router_weight.T, rows_map, lanes_map
    )
    arrived = chips(outgoing)
    produced = expert_part(arrived, expert_first, expert_second, first_other, second_other)
    return combine_part(residual, wide, chips(produced))


def solution(mesh):
    fine = Mesh(mesh.devices.reshape(4, 4, 4, 2), ("x", "z", "y", "c"))
    head = ("z", "y", "c")
    every = ("x", "z", "y", "c")
    in_specs = (
        P("x", None),
        P(),
        P(None, None, head),
        P(None, head),
        P(head, None),
        P(),
        P(),
        P(every, None),
        P(None, None, every),
        P(every, None),
    )
    return jax.shard_map(body, mesh=fine, in_specs=in_specs, out_specs=P(every, None), check_vma=False)
```

```python
import math

import jax
import jax.numpy as jnp
from jax import lax
from jax.experimental import pallas as pl
from jax.experimental.pallas import tpu as pltpu
from jax.sharding import Mesh
from jax.sharding import PartitionSpec as P

HD = 128
D = 2048
STATE = 8256
EXPERTS = 64
TOP = 8
CAP = 3
SLAB = 16
HALF = 256
SHARD = 512
CHIP_AXES = ("x", "z", "y")


def swap_core(array):
    return lax.ppermute(array, "c", [(0, 1), (1, 0)])


def pair(array, axis, bits):
    return lax.ppermute(array, axis, [(i, i ^ bits) for i in range(4)])


def shift(array, axis, step):
    return lax.ppermute(array, axis, [(i, (i + step) % 4) for i in range(4)])


VMEM = pl.BlockSpec(memory_space=pltpu.VMEM)


def room(mebibytes):
    return pltpu.CompilerParams(vmem_limit_bytes=int(mebibytes * 1024 * 1024))


def cost(microseconds):
    return pl.CostEstimate(
        flops=int(microseconds * 1e9), bytes_accessed=int(microseconds * 3e6), transcendentals=0
    )


ROWS = EXPERTS * CAP
PIECES = D // 128
TILE_ROWS = ROWS * PIECES


def norm_scaled(values, gain):
    return values * lax.rsqrt(jnp.mean(values * values, axis=-1, keepdims=True) + 1e-06) * gain


GROUP = 8
TAIL_AT = 8064


def carried_kernel(m_ref, q_own_ref, q_other_ref, out_ref, q_ref, w_a, w_b, tail_ref):
    tail_ref[:, : STATE - TAIL_AT] = m_ref[:, TAIL_AT:]
    q_ref[:, :HALF] = q_own_ref[...].astype(jnp.float32)
    q_ref[:, HALF:] = q_other_ref[...].astype(jnp.float32)
    q_cols = jnp.concatenate([q_own_ref[...], q_other_ref[...]], axis=1)
    lane = lax.broadcasted_iota(jnp.int32, (64, 128), 1)
    root = math.sqrt(2.0)
    weights = (w_a, w_b)

    def prepare(number):
        base = number * GROUP
        for k in range(GROUP):
            i = base + k
            offset = 127 * i - (i * (i - 1)) // 2
            tile, turn = (offset // 128) * 128, offset % 128
            if tile < TAIL_AT:
                first, second = m_ref[:, tile : tile + 128], m_ref[:, tile + 128 : tile + 256]
            else:
                first, second = tail_ref[:, :128], tail_ref[:, 128:]
            if turn == 0:
                joined = first
            else:
                joined = jnp.where(
                    lane < 128 - turn,
                    pltpu.roll(first, 128 - turn, 1),
                    pltpu.roll(second, 128 - turn, 1),
                )
            weights[number % 2][64 * k : 64 * k + 64, :] = jnp.where(
                lane > i, joined * root, jnp.where(lane == i, joined, 0.0)
            ).astype(jnp.bfloat16)

    prepare(0)
    for number in range(HD // GROUP):
        spread = jnp.dot(weights[number % 2][...], q_cols, preferred_element_type=jnp.float32)
        if number + 1 < HD // GROUP:
            prepare(number + 1)
        base = number * GROUP
        total = spread[0:64] * q_ref[base : base + 1, :]
        for k in range(1, GROUP):
            total = total + spread[64 * k : 64 * k + 64] * q_ref[base + k : base + k + 1, :]
        if number == 0:
            out_ref[...] = total
        else:
            out_ref[...] += total


def carried_part(state_cols, q_own, q_other):
    return pl.pallas_call(
        carried_kernel,
        out_shape=jax.ShapeDtypeStruct((64, SHARD), jnp.float32),
        in_specs=[VMEM] * 3,
        out_specs=VMEM,
        scratch_shapes=[
            pltpu.VMEM((HD, SHARD), jnp.float32),
            pltpu.VMEM((64 * GROUP, HD), jnp.bfloat16),
            pltpu.VMEM((64 * GROUP, HD), jnp.bfloat16),
            pltpu.VMEM((64, 256), jnp.float32),
        ],
        compiler_params=room(2),
        cost_estimate=cost(5),
        name="carried",
    )(state_cols, q_own, q_other)


def window_kernel(q_own_ref, q_other_ref, kv0, kv1, kv2, kv3, carried_ref, mine_ref, send_ref):
    core, shard = lax.axis_index("c"), lax.axis_index("x")
    q_cols = jnp.concatenate([q_own_ref[...], q_other_ref[...]], axis=1)
    key = lax.broadcasted_iota(jnp.int32, (HALF, SHARD), 0)
    query = lax.broadcasted_iota(jnp.int32, (HALF, SHARD), 1)
    key_place = (key // 16) * 32 + key % 16 + core * 16
    inside = query % HALF
    query_place = (inside // 16) * 32 + inside % 16 + jnp.where(query < HALF, core, 1 - core) * 16
    allowed = key_place <= query_place
    total = jnp.zeros((HD, SHARD), jnp.float32)
    for number, kv in enumerate((kv0, kv1, kv2, kv3)):
        scores = lax.dot_general(
            kv[:HD, :], q_cols, (((0,), (0,)), ((), ())), preferred_element_type=jnp.float32
        )
        weights = scores * scores
        if number == 0:
            weights = jnp.where(allowed, weights, 0.0)
        else:
            weights = jnp.where((shard ^ number) < shard, weights, 0.0)
        total = total + jnp.dot(
            kv[HD:, :], weights.astype(jnp.bfloat16), preferred_element_type=jnp.float32
        )
    upper = total[:64] + carried_ref[...]
    lower = total[64:]
    mine_ref[...] = jnp.concatenate([upper[:, :HALF], lower[:, :HALF]], axis=0).T
    send_ref[...] = jnp.concatenate([lower[:, HALF:], upper[:, HALF:]], axis=0).T.astype(jnp.bfloat16)


def window_part(q_own, q_other, kvs, carried):
    return pl.pallas_call(
        window_kernel,
        out_shape=(
            jax.ShapeDtypeStruct((HALF, HD), jnp.float32),
            jax.ShapeDtypeStruct((HALF, HD), jnp.bfloat16),
        ),
        in_specs=[VMEM] * 7,
        out_specs=(VMEM,) * 2,
        compiler_params=room(2),
        cost_estimate=cost(2),
        name="window",
    )(q_own, q_other, *kvs, carried)


def norm_kernel(tokens_ref, out_ref, slab_ref):
    core = lax.axis_index("c")
    slab_ref[...] = tokens_ref[lax.axis_index("z") * 4 + lax.axis_index("y"), core]
    for k in range(4):
        floats = tokens_ref[4 * k : 4 * k + 4, core].astype(jnp.float32).reshape(64, D)
        out_ref[64 * k : 64 * k + 64, :] = norm_scaled(floats, 1.0)


def norm_part(tokens):
    return pl.pallas_call(
        norm_kernel,
        out_shape=(
            jax.ShapeDtypeStruct((HALF, D), jnp.float32),
            jax.ShapeDtypeStruct((SLAB, D), jnp.bfloat16),
        ),
        in_specs=[VMEM],
        out_specs=(VMEM, VMEM),
        compiler_params=room(2),
        cost_estimate=cost(1),
        name="norm",
    )(tokens.reshape(16, 2, 16, D))


def project_kernel(normed_ref, gain_ref, own_ref, other_ref, q_ref, kv_ref):
    core = lax.axis_index("c")
    normed = (normed_ref[...] * gain_ref[...]).astype(jnp.bfloat16)

    def times(ref):
        return lax.dot_general(
            ref[...].reshape(192, D),
            normed,
            (((1,), (1,)), ((), ())),
            preferred_element_type=jnp.float32,
        ).astype(jnp.bfloat16)

    own, other = times(own_ref), times(other_ref)
    own_at = pl.multiple_of(core * 64, 64)
    other_at = pl.multiple_of((1 - core) * 64, 64)
    q_ref[pl.ds(own_at, 64), :] = own[:64]
    q_ref[pl.ds(other_at, 64), :] = other[:64]
    kv_ref[pl.ds(own_at, 64), :] = own[64:128]
    kv_ref[pl.ds(other_at, 64), :] = other[64:128]
    kv_ref[128:192, :] = own[128:]
    kv_ref[192:256, :] = other[128:]


def project_part(normed, gain, own, other):
    return pl.pallas_call(
        project_kernel,
        out_shape=(
            jax.ShapeDtypeStruct((HD, HALF), jnp.bfloat16),
            jax.ShapeDtypeStruct((2 * HD, HALF), jnp.bfloat16),
        ),
        in_specs=[VMEM] * 4,
        out_specs=(VMEM, VMEM),
        compiler_params=room(4),
        cost_estimate=cost(1),
        name="project",
    )(normed, gain.reshape(1, D), own, other)


def attend_kernel(mine_ref, received_ref, keep_ref, first_ref, second_ref, scratch):
    raw = (mine_ref[...] + received_ref[...].astype(jnp.float32)) / HD
    scratch[...] = norm_scaled(raw, 1.0).reshape(4, 64, HD)

    def block(bits):
        at = pl.multiple_of((lax.axis_index("y") ^ bits) * SLAB, SLAB)
        return scratch[:, pl.ds(at, SLAB), :].reshape(64, HD).astype(jnp.bfloat16)

    keep_ref[...] = block(0)
    first_ref[:64, :] = block(1)
    first_ref[64:, :] = block(2)
    second_ref[...] = block(3)


def attend_part(mine, received):
    return pl.pallas_call(
        attend_kernel,
        out_shape=(
            jax.ShapeDtypeStruct((64, HD), jnp.bfloat16),
            jax.ShapeDtypeStruct((128, HD), jnp.bfloat16),
            jax.ShapeDtypeStruct((64, HD), jnp.bfloat16),
        ),
        in_specs=[VMEM, VMEM],
        out_specs=(VMEM,) * 3,
        scratch_shapes=[pltpu.VMEM((4, 64, HD), jnp.float32)],
        compiler_params=room(2),
        cost_estimate=cost(0.7),
        name="attend",
    )(mine, received)


def relay_kernel(own_ref, received_ref, out_ref):
    out_ref[:64, :] = own_ref[...]
    out_ref[64:, :] = received_ref[64:, :]


def relay_part(own, received):
    return pl.pallas_call(
        relay_kernel,
        out_shape=jax.ShapeDtypeStruct((128, HD), jnp.bfloat16),
        in_specs=[VMEM, VMEM],
        out_specs=VMEM,
        compiler_params=room(2),
        cost_estimate=cost(0.2),
        name="relay",
    )(own, received)


def pack_kernel(*refs):
    for step in range(4):
        refs[4][64 * step : 64 * step + 64, :] = refs[step][...]


def pack_part(rows):
    return pl.pallas_call(
        pack_kernel,
        out_shape=jax.ShapeDtypeStruct((HALF, D), jnp.bfloat16),
        in_specs=[VMEM] * 4,
        out_specs=VMEM,
        compiler_params=room(2),
        cost_estimate=cost(0.5),
        name="pack",
    )(*rows)


def output_kernel(*rest):
    pieces, own, other, outs, scratch = rest[:3], rest[3], rest[4], rest[5:9], rest[9]
    loaded = [pieces[0][...], pieces[1][:64, :], pieces[2][:64, :], pieces[2][64:, :]]
    for at in range(0, D, 512):
        total = jnp.zeros((64, 512), jnp.float32)
        for step in range(4):
            total = total + jnp.dot(
                loaded[step][:, :64],
                own[64 * step : 64 * step + 64, at : at + 512],
                preferred_element_type=jnp.float32,
            )
            total = total + jnp.dot(
                loaded[step][:, 64:],
                other[64 * step : 64 * step + 64, at : at + 512],
                preferred_element_type=jnp.float32,
            )
        scratch[:, at : at + 512] = total
    for step, out in enumerate(outs):
        at = pl.multiple_of(lax.rem(lax.axis_index("z") + step, 4) * SLAB, SLAB)
        out[...] = scratch[pl.ds(at, SLAB), :].astype(out.dtype)


def output_part(pieces, own, other):
    return pl.pallas_call(
        output_kernel,
        out_shape=(jax.ShapeDtypeStruct((SLAB, D), jnp.float32),)
        + (jax.ShapeDtypeStruct((SLAB, D), jnp.bfloat16),) * 3,
        in_specs=[VMEM] * 5,
        out_specs=(VMEM,) * 4,
        scratch_shapes=[pltpu.VMEM((64, D), jnp.float32)],
        compiler_params=room(2),
        cost_estimate=cost(2),
        name="output",
    )(*pieces, own, other)


def map_kernel(index_ref, gain_ref, rows_ref, lanes_ref, gain_out):
    gain_out[...] = gain_ref[...]
    index = index_ref[...]
    expert = lax.broadcasted_iota(jnp.int32, (EXPERTS, SLAB), 0)
    chosen = jnp.zeros((EXPERTS, SLAB), jnp.float32)
    for k in range(TOP):
        chosen = chosen + jnp.where(index[k : k + 1, :] == expert, 1.0, 0.0)
    before = lax.broadcasted_iota(jnp.int32, (SLAB, SLAB), 0) < lax.broadcasted_iota(
        jnp.int32, (SLAB, SLAB), 1
    )
    slot = jnp.dot(
        chosen.astype(jnp.bfloat16),
        jnp.where(before, 1.0, 0.0).astype(jnp.bfloat16),
        preferred_element_type=jnp.float32,
    )
    code = jnp.where(chosen > 0.5, slot, -1.0).astype(jnp.bfloat16)
    lane = lax.broadcasted_iota(jnp.int32, (SLAB, TILE_ROWS), 1)
    wide = lax.dot_general(
        code, spread_map(), (((0,), (0,)), ((), ())), preferred_element_type=jnp.float32
    )
    lanes_ref[...] = jnp.where(
        wide == ((lane // PIECES) % CAP).astype(jnp.float32), 1.0, 0.0
    )
    token = lax.broadcasted_iota(jnp.int32, (SLAB, 256), 0)
    column = lax.broadcasted_iota(jnp.int32, (SLAB, 256), 1)
    by_column = jnp.dot(
        code,
        jnp.where(column % SLAB == token, 1.0, 0.0).astype(jnp.bfloat16),
        preferred_element_type=jnp.float32,
    ).astype(jnp.bfloat16)
    row_expert = lax.broadcasted_iota(jnp.int32, (TILE_ROWS, EXPERTS), 0) // (CAP * PIECES)
    pick = jnp.where(
        row_expert == lax.broadcasted_iota(jnp.int32, (TILE_ROWS, EXPERTS), 1), 1.0, 0.0
    ).astype(jnp.bfloat16)
    tall = jnp.dot(pick, by_column, preferred_element_type=jnp.float32)
    row = lax.broadcasted_iota(jnp.int32, (TILE_ROWS, 256), 0)
    piece = lax.broadcasted_iota(jnp.int32, (TILE_ROWS, 256), 1) // SLAB
    rows_ref[...] = jnp.where(
        (tall == ((row // PIECES) % CAP).astype(jnp.float32)) & (row % PIECES == piece), 1.0, 0.0
    ).astype(jnp.bfloat16)


def spread_map():
    lane_expert = lax.broadcasted_iota(jnp.int32, (EXPERTS, TILE_ROWS), 1) // (CAP * PIECES)
    return jnp.where(
        lane_expert == lax.broadcasted_iota(jnp.int32, (EXPERTS, TILE_ROWS), 0), 1.0, 0.0
    ).astype(jnp.bfloat16)


def map_part(index, gain):
    return pl.pallas_call(
        map_kernel,
        out_shape=(
            jax.ShapeDtypeStruct((TILE_ROWS, 256), jnp.bfloat16),
            jax.ShapeDtypeStruct((SLAB, TILE_ROWS), jnp.float32),
            jax.ShapeDtypeStruct((1, D), jnp.float32),
        ),
        in_specs=[VMEM, VMEM],
        out_specs=(VMEM,) * 3,
        compiler_params=room(14),
        cost_estimate=cost(2),
        name="maps",
    )(index, gain.reshape(1, D))


def dispatch_kernel(
    slab_ref, own_ref, r1, r2, r3, gain_ref, router_ref, rows_ref, lanes_ref, residual_ref, out_ref, wide_ref
):
    residual = slab_ref[...].astype(jnp.float32) + own_ref[...]
    for received in (r1, r2, r3):
        residual = residual + received[...].astype(jnp.float32)
    residual_ref[...] = residual
    inputs = norm_scaled(residual, gain_ref[...]).astype(jnp.bfloat16)
    logits = lax.dot_general(
        inputs, router_ref[...], (((1,), (1,)), ((), ())), preferred_element_type=jnp.float32
    )
    wide_ref[...] = lanes_ref[...] * jnp.dot(
        jax.nn.sigmoid(logits).astype(jnp.bfloat16),
        spread_map(),
        preferred_element_type=jnp.float32,
    )
    tall = jnp.concatenate([inputs[:, at : at + 128] for at in range(0, D, 128)], axis=0)
    out_ref[...] = jnp.dot(rows_ref[...], tall, preferred_element_type=jnp.float32).astype(
        jnp.bfloat16
    )


def dispatch_part(slab, own, received, gain, router, rows, lanes):
    return pl.pallas_call(
        dispatch_kernel,
        out_shape=(
            jax.ShapeDtypeStruct((SLAB, D), jnp.float32),
            jax.ShapeDtypeStruct((TILE_ROWS, 128), jnp.bfloat16),
            jax.ShapeDtypeStruct((SLAB, TILE_ROWS), jnp.float32),
        ),
        in_specs=[VMEM] * 9,
        out_specs=(VMEM,) * 3,
        compiler_params=room(6),
        cost_estimate=cost(1),
        name="dispatch",
    )(slab, own, *received, gain, router, rows, lanes)


def expert_kernel(
    rows_ref, first_own, second_own, first_other, second_other, out_ref, flat_ref, input_ref, total_ref
):
    flat_ref[...] = rows_ref[...].astype(jnp.float32)
    for at in range(PIECES):
        input_ref[:, at * 128 : (at + 1) * 128] = flat_ref[
            pl.ds(at, ROWS, stride=PIECES), :
        ].astype(jnp.bfloat16)
    for piece, (first, second) in enumerate(
        ((first_own, second_own), (first_other, second_other))
    ):
        gate = jnp.dot(input_ref[...], first[0], preferred_element_type=jnp.float32)
        up = jnp.dot(input_ref[...], first[1], preferred_element_type=jnp.float32)
        hidden = (gate / (1.0 + jnp.exp(-gate)) * up).astype(jnp.bfloat16)
        product = jnp.dot(hidden, second[...], preferred_element_type=jnp.float32)
        if piece == 0:
            total_ref[...] = product
        else:
            product = product + total_ref[...]
            for at in range(PIECES):
                flat_ref[pl.ds(at, ROWS, stride=PIECES), :] = product[:, at * 128 : (at + 1) * 128]
    out_ref[...] = flat_ref[...].astype(jnp.bfloat16)


def expert_part(rows, first, second, first_other, second_other):
    return pl.pallas_call(
        expert_kernel,
        out_shape=jax.ShapeDtypeStruct((TILE_ROWS, 128), jnp.bfloat16),
        in_specs=[VMEM] * 5,
        out_specs=VMEM,
        scratch_shapes=[
            pltpu.VMEM((TILE_ROWS, 128), jnp.float32),
            pltpu.VMEM((ROWS, D), jnp.bfloat16),
            pltpu.VMEM((ROWS, D), jnp.float32),
        ],
        compiler_params=room(28),
        cost_estimate=cost(5),
        name="experts",
    )(rows, first, second, first_other, second_other)


def combine_kernel(residual_ref, wide_ref, rows_ref, out_ref, map_ref):
    wide = wide_ref[...]
    piece = lax.broadcasted_iota(jnp.int32, (SLAB, TILE_ROWS), 1) % PIECES
    for at in range(PIECES):
        map_ref[at * SLAB : (at + 1) * SLAB, :] = jnp.where(piece == at, wide, 0.0).astype(
            jnp.bfloat16
        )
    tall = jnp.dot(map_ref[...], rows_ref[...], preferred_element_type=jnp.float32)
    for at in range(PIECES):
        columns = slice(at * 128, (at + 1) * 128)
        out_ref[:, columns] = (
            residual_ref[:, columns] + tall[at * SLAB : (at + 1) * SLAB, :]
        ).astype(jnp.bfloat16)


def combine_part(residual, wide, rows):
    return pl.pallas_call(
        combine_kernel,
        out_shape=jax.ShapeDtypeStruct((SLAB, D), jnp.bfloat16),
        in_specs=[VMEM] * 3,
        out_specs=VMEM,
        scratch_shapes=[pltpu.VMEM((256, TILE_ROWS), jnp.bfloat16)],
        compiler_params=room(6),
        cost_estimate=cost(1),
        name="combine",
    )(residual, wide, rows)


def chips(rows):
    shaped = rows.reshape(EXPERTS, CAP * PIECES, 128)
    return lax.all_to_all(shaped, CHIP_AXES, split_axis=0, concat_axis=0, tiled=True).reshape(
        TILE_ROWS, 128
    )


def body(
    tokens,
    attention_gain,
    head_weights,
    carried_state,
    output_weight,
    expert_gain,
    router_weight,
    expert_index,
    expert_first,
    expert_second,
):
    own_weights = head_weights.transpose(0, 2, 1)
    other_weights = swap_core(own_weights)
    output_near = pair(output_weight, "y", 1)
    output_own = [output_weight, output_near, pair(output_weight, "y", 3), pair(output_near, "y", 3)]
    normed, slab = norm_part(tokens)
    q_own, kv = project_part(normed, attention_gain, own_weights, other_weights)
    kv_near = pair(kv, "x", 1)
    kvs = [kv, kv_near, pair(kv_near, "x", 3), pair(kv, "x", 3)]
    q_other = swap_core(q_own)
    rows_map, lanes_map, gain = map_part(expert_index.T, expert_gain)

    carried = carried_part(carried_state.T, q_own, q_other)
    mine, send = window_part(q_own, q_other, kvs, carried)
    tied = lax.optimization_barrier((swap_core(send), expert_first, expert_second, *output_own))
    received, output_own = tied[0], pack_part(tied[3:])
    first_other, second_other = swap_core(tied[1]), swap_core(tied[2])
    output_other = swap_core(output_own)
    kept, first, second = attend_part(mine, received)
    first = pair(first, "y", 1)
    second = pair(relay_part(second, first), "y", 3)
    sums = output_part((kept, first, second), output_own, output_other)
    summed = [shift(sums[step], "z", step) for step in (1, 2, 3)]
    residual, outgoing, wide = dispatch_part(
        slab, sums[0], summed, gain, router_weight.T, rows_map, lanes_map
    )
    arrived = chips(outgoing)
    produced = expert_part(arrived, expert_first, expert_second, first_other, second_other)
    return combine_part(residual, wide, chips(produced))


def solution(mesh):
    fine = Mesh(mesh.devices.reshape(4, 4, 4, 2), ("x", "z", "y", "c"))
    head = ("z", "y", "c")
    every = ("x", "z", "y", "c")
    in_specs = (
        P("x", None),
        P(),
        P(None, None, head),
        P(None, head),
        P(head, None),
        P(),
        P(),
        P(every, None),
        P(None, None, every),
        P(every, None),
    )
    return jax.shard_map(body, mesh=fine, in_specs=in_specs, out_specs=P(every, None), check_vma=False)
```
